32 devices in a mesh: ctx: 2 (over x), head: 4 (over z), roll: 4 (over y, core).
Axes of the slice: x: 2, y: 2, z: 4, core: 2. Of those that a mesh axis runs over, the one named last changes fastest.
Arguments:
- queries: bfloat16 [4, 8, 256, 128], P('roll', 'head', 'ctx'), may hold values from -80 to 80
- cache_keys: bfloat16 [4, 8, 6144, 128], P('roll', 'head', 'ctx'), may hold values from -4.5 to 4.5
- cache_values: bfloat16 [4, 8, 6144, 128], P('roll', 'head', 'ctx'), may hold values from -6 to 6
- new_keys: bfloat16 [4, 8, 16, 128], P('roll', 'head'), may hold values from -12 to 12
- new_values: bfloat16 [4, 8, 16, 128], P('roll', 'head'), may hold values from -6 to 6
- lengths: int32 [4], P('roll'), may hold values from 3072 to 6144, as said below
- positions: int32 [4, 16], P('roll'), may hold values from 3072 to 6159, as said below
- out_weight: bfloat16 [16384, 16384], P('head', ('ctx', 'roll')), may hold values from -0.046875 to 0.046875
Outputs:
- projected: bfloat16 [4, 16, 16384], P('head', None, ('ctx', 'roll'))
The draws below stay inside these ranges and needn't reach their ends.
Inputs may be any that keep to these rules, and one draw needn't show every extreme that they name: `lengths`: at least one rollout has the full 6144 slots. positions[r] is lengths[r] plus a permutation of 0 .. 15.
All inputs are finite; a program needn't handle non-finite values.
Results may differ from the reference program's by a relative error of at most 0.04.
Values may be sent and summed in bfloat16 or wider, within the bound.
A program may use at most 64 MiB of HBM per device.

```python
import jax
import jax.numpy as jnp
from jax import lax

D = 16384
QH = 128
KVH = 8
DH = 128
NEW = 16
QPK = 16
CACHE = 6144
ROLL = 4


def shared_keys(key):
    base = jax.random.fold_in(key, 11)
    return jnp.clip(jax.random.normal(base, (ROLL, KVH, CACHE, DH), jnp.float32), -4.5, 4.5)


def rollout_bounds(key):
    lengths = jax.random.randint(jax.random.fold_in(key, 21), (ROLL,), CACHE // 2, CACHE + 1)
    filled = jax.random.randint(jax.random.fold_in(key, 22), (), 0, ROLL)
    lengths = jnp.where(jnp.arange(ROLL) == filled, CACHE, lengths).astype(jnp.int32)
    orders = jax.vmap(lambda sub: jax.random.permutation(sub, NEW))(jax.random.split(jax.random.fold_in(key, 23), ROLL))
    positions = lengths[:, None] + orders.astype(jnp.int32)
    return (lengths, positions.astype(jnp.int32))


def draw_cache_keys(key, part):
    keys = shared_keys(key)
    return keys.astype(jnp.bfloat16)


def draw_queries(key, part):
    key = jax.random.fold_in(key, 2)
    rows = NEW * QPK
    values = 3.0 * jnp.clip(jax.random.normal(key, (ROLL, KVH, rows, DH), jnp.float32), -4.0, 4.0)
    return values.astype(jnp.bfloat16)


def draw_lengths(key, part):
    lengths, positions = rollout_bounds(key)
    return lengths


def draw_positions(key, part):
    lengths, positions = rollout_bounds(key)
    return positions


def block_scale(key, extent, shards, smallest, largest):
    def one(axis_at, blocks):
        steps = jax.random.uniform(jax.random.fold_in(jax.random.fold_in(key, 6), axis_at), (blocks,), jnp.float32, smallest / len(shards), largest / len(shards))
        return jnp.repeat(jnp.exp(steps), extent[axis_at] // blocks).reshape((-1,) + (1,) * (len(extent) - axis_at - 1))

    level = one(*shards[0])
    for cut in shards[1:]:
        level = level * one(*cut)
    return level


def normal_values(rng, extent, width, limit, pieces=(), kind=jnp.bfloat16):
    array = jax.random.normal(rng, extent, jnp.float32) * width
    if len(pieces) > 0:
        array = block_scale(rng, extent, pieces, -0.22, 0.18) * array
    return jnp.clip(array, min=-limit, max=limit).astype(kind)


def setup_inputs(seed: int = 0) -> dict:
    key_of = jax.random.split(jax.random.key(seed), 9)
    return {
        "queries": draw_queries(jax.random.fold_in(key_of[8], 71), 0),
        "cache_keys": draw_cache_keys(jax.random.fold_in(key_of[8], 71), 0),
        "cache_values": normal_values(key_of[2], (ROLL, KVH, CACHE, DH), 1.0, 6.0, ((0, 4), (1, 4), (2, 2))),
        "new_keys": normal_values(key_of[3], (ROLL, KVH, NEW, DH), 2.5, 12.0, ((0, 4), (1, 4))),
        "new_values": normal_values(key_of[4], (ROLL, KVH, NEW, DH), 1.0, 6.0, ((0, 4), (1, 4))),
        "lengths": draw_lengths(jax.random.fold_in(key_of[8], 71), 0),
        "positions": draw_positions(jax.random.fold_in(key_of[8], 71), 0),
        "out_weight": normal_values(key_of[7], (QH * DH, D), (QH * DH) ** -0.5, 0.046875, ((0, 4), (1, 8))),
    }


NEG = -1.0e30


def attend_one(items):
    query, keys, values, fresh_keys, fresh_values, length, pos = items
    scale = 1.0 / (DH ** 0.5)
    scores = jnp.dot(query, keys.T, preferred_element_type=jnp.float32) * scale
    keep = jnp.arange(CACHE) < length
    scores = jnp.where(keep[None, :], scores, NEG)
    fresh = jnp.dot(query, fresh_keys.T, preferred_element_type=jnp.float32) * scale
    token = jnp.arange(NEW * QPK) // QPK
    allow = pos[None, :] <= pos[token][:, None]
    fresh = jnp.where(allow, fresh, NEG)
    top = jnp.maximum(jnp.max(scores, axis=1), jnp.max(fresh, axis=1))
    cache_weights = jnp.where(keep[None, :], jnp.exp(scores - top[:, None]), 0.0).astype(jnp.bfloat16)
    fresh_weights = jnp.where(allow, jnp.exp(fresh - top[:, None]), 0.0).astype(jnp.bfloat16)
    total = jnp.sum(cache_weights.astype(jnp.float32), axis=1) + jnp.sum(fresh_weights.astype(jnp.float32), axis=1)
    summed = jnp.dot(cache_weights, values, preferred_element_type=jnp.float32)
    summed = summed + jnp.dot(fresh_weights, fresh_values, preferred_element_type=jnp.float32)
    return (summed / total[:, None]).astype(jnp.bfloat16)


def reference(queries, cache_keys, cache_values, new_keys, new_values, lengths, positions, out_weight):
    flat = ROLL * KVH
    items = (
        queries.reshape(flat, NEW * QPK, DH),
        cache_keys.reshape(flat, CACHE, DH),
        cache_values.reshape(flat, CACHE, DH),
        new_keys.reshape(flat, NEW, DH),
        new_values.reshape(flat, NEW, DH),
        jnp.repeat(lengths, KVH),
        jnp.repeat(positions, KVH, axis=0),
    )
    attended = lax.map(attend_one, items)
    attended = attended.reshape(ROLL, KVH, NEW, QPK, DH).transpose(0, 2, 1, 3, 4)
    features = attended.reshape(ROLL * NEW, QH * DH)
    projected = jnp.dot(features, out_weight, preferred_element_type=jnp.float32)
    return projected.astype(jnp.bfloat16).reshape(ROLL, NEW, D)
```

```python
import functools
import math

import jax
import jax.numpy as jnp
from jax import lax
from jax.experimental import pallas as pl
from jax.experimental.pallas import tpu as pltpu
from jax.sharding import PartitionSpec as P

NEW = 16
QPK = 16


NEG = -1e30

MESH = pl.DeviceIdType.MESH
CHUNK = 512
COLS = 512
WCUT = 4


def fused_kernel(
    n_head,
    q_hbm, k_hbm, v_hbm, fk_hbm, fv_hbm, len_ref, pos_ref, w_hbm,
    out_ref,
    qbuf, kbuf, vbuf, fkbuf, fvbuf, wbuf, sbuf,
    po_send, po_recv, st_send, st_recv, fbuf, gather, accbuf, rs_send, rs_recv,
    q_sem, k_sem, v_sem, f_sem, w_sem,
    qx_send, qx_recv, px_send, px_recv, sx_send, sx_recv,
    g_send, g_recv, rs_send_sem, rs_recv_sem,
):
    f32, bf16 = jnp.float32, jnp.bfloat16
    c, h, r = lax.axis_index("ctx"), lax.axis_index("head"), lax.axis_index("roll")
    other = 1 - c
    sib = r + 1 - 2 * lax.rem(r, 2)
    far = lax.rem(r + 2, 4)
    far_sib = lax.rem(sib + 2, 4)
    partner = {"ctx": other}
    rows, head_size = qbuf.shape[1], qbuf.shape[2]
    half = rows // 2
    slots = kbuf.shape[1]
    factor = math.log2(math.e) / math.sqrt(head_size)

    barrier = pltpu.get_barrier_semaphore()
    peers = [partner, {"roll": sib}, {"roll": far}, {"ctx": other, "roll": far}]
    peers += [{"head": lax.rem(h + off, n_head)} for off in range(1, n_head)]
    for peer in peers:
        pl.semaphore_signal(barrier, inc=1, device_id=peer, device_id_type=MESH)

    local = {}

    def fetch(name, src, dst, sem):
        local[name] = pltpu.make_async_copy(src, dst, sem)
        local[name].start()

    mine = pl.ds(pl.multiple_of(c * half, half), half)
    fetch("q", q_hbm.at[0], qbuf.at[:, mine, :], q_sem)
    fetch("k0", k_hbm.at[0, other], kbuf.at[other], k_sem.at[0])
    fetch("v0", v_hbm.at[0, other], vbuf.at[other], v_sem.at[0])
    fetch("k1", k_hbm.at[0, c], kbuf.at[c], k_sem.at[1])
    fetch("v1", v_hbm.at[0, c], vbuf.at[c], v_sem.at[1])
    fetch("fk", fk_hbm.at[0, c], fkbuf, f_sem.at[0])
    fetch("fv", fv_hbm.at[0, c], fvbuf, f_sem.at[1])

    pl.semaphore_wait(barrier, len(peers))

    q_copies = []
    for at, head in enumerate((c, other)):
        q_copies.append(
            pltpu.make_async_remote_copy(
                src_ref=q_hbm.at[0, head],
                dst_ref=qbuf.at[head, mine, :],
                send_sem=qx_send.at[at],
                recv_sem=qx_recv.at[at],
                device_id=partner,
                device_id_type=MESH,
            )
        )
        q_copies[-1].start()

    depth = w_hbm.shape[0] // 2
    piece = depth // WCUT
    for at, head in enumerate((c, other)):
        for cut in range(WCUT):
            fetch(
                ("w", at, cut),
                w_hbm.at[pl.ds(pl.multiple_of(head * depth + cut * piece, piece), piece), :],
                wbuf.at[head, pl.ds(cut * piece, piece), :],
                w_sem.at[at, cut],
            )

    length = len_ref[0]
    first_slot = c * slots

    def scores(query, head):
        fold = jnp.full((query.shape[0], 128), NEG, f32)
        for at in range(slots // CHUNK):
            span = slice(at * CHUNK, (at + 1) * CHUNK)
            part = lax.dot_general(
                query, kbuf[head, span, :], (((1,), (1,)), ((), ())), preferred_element_type=f32
            )
            slot = first_slot + at * CHUNK + lax.broadcasted_iota(jnp.int32, (1, CHUNK), 1)
            part = part + jnp.where(slot < length, 0.0, NEG)
            sbuf[0 : query.shape[0], span] = part
            for lane in range(CHUNK // 128):
                fold = jnp.maximum(fold, part[:, lane * 128 : (lane + 1) * 128])
        return jnp.max(fold, axis=1, keepdims=True)

    def weighted(count, head, top):
        ones = jnp.ones((CHUNK, 128), bf16)
        acc = jnp.zeros((count, head_size + 128), f32)
        for at in range(slots // CHUNK):
            span = slice(at * CHUNK, (at + 1) * CHUNK)
            weights = jnp.exp2((sbuf[0:count, span] - top) * factor).astype(bf16)
            both = jnp.concatenate([vbuf[head, span, :], ones], axis=1)
            acc = acc + jnp.dot(weights, both, preferred_element_type=f32)
        return acc[:, :head_size], acc[:, head_size:]

    lane = lax.broadcasted_iota(jnp.int32, (half, 128), 1)
    p_copies, s_copies = [], []
    for at, side in enumerate((c, other)):
        if at == 0:
            local["q"].wait()
            local["k0"].wait()
        else:
            q_copies[0].wait_recv()
        query = qbuf[other, pl.ds(pl.multiple_of(side * half, half), half), :]
        top = scores(query, other)
        if at == 0:
            local["v0"].wait()
        summed, total = weighted(half, other, top)
        po_send[side] = summed.astype(bf16)
        turned = jnp.transpose(jnp.where(lane < 64, jnp.broadcast_to(top, (half, 128)), total))
        st_send[side, 0:8, :] = turned[0:8, :]
        st_send[side, 8:16, :] = turned[64:72, :]
        p_copies.append(
            pltpu.make_async_remote_copy(
                src_ref=po_send.at[side], dst_ref=po_recv.at[side],
                send_sem=px_send.at[at], recv_sem=px_recv.at[at],
                device_id=partner, device_id_type=MESH,
            )
        )
        s_copies.append(
            pltpu.make_async_remote_copy(
                src_ref=st_send.at[side], dst_ref=st_recv.at[side],
                send_sem=sx_send.at[at], recv_sem=sx_recv.at[at],
                device_id=partner, device_id_type=MESH,
            )
        )
        p_copies[-1].start()
        s_copies[-1].start()

    token = lax.broadcasted_iota(jnp.int32, (rows, NEW), 0) // QPK
    fresh_at = lax.broadcasted_iota(jnp.int32, (rows, NEW), 1)
    row_pos = jnp.zeros((rows, NEW), jnp.int32)
    new_pos = jnp.zeros((rows, NEW), jnp.int32)
    for t in range(NEW):
        value = pos_ref[0, t]
        row_pos = jnp.where(token == t, value, row_pos)
        new_pos = jnp.where(fresh_at == t, value, new_pos)
    allow = new_pos <= row_pos

    q_copies[1].wait_recv()
    local["k1"].wait()
    local["fk"].wait()
    query = qbuf[c]
    top = scores(query, c)
    fresh = lax.dot_general(
        query, fkbuf[...], (((1,), (1,)), ((), ())), preferred_element_type=f32
    )
    fresh = jnp.where(allow, fresh, NEG)
    top = jnp.maximum(top, jnp.max(fresh, axis=1, keepdims=True))
    local["v1"].wait()
    local["fv"].wait()
    summed, total = weighted(rows, c, top)
    fresh_weights = jnp.where(allow, jnp.exp2((fresh - top) * factor), 0.0).astype(bf16)
    summed = summed + jnp.dot(fresh_weights, fvbuf[...], preferred_element_type=f32)
    total = total + jnp.sum(fresh_weights.astype(f32), axis=1, keepdims=True)

    for copy in p_copies + s_copies:
        copy.wait_recv()
    for side in range(2):
        span = slice(side * half, (side + 1) * half)
        top_here = jnp.broadcast_to(top[span], (half, 128))
        top_there = jnp.transpose(jnp.broadcast_to(st_recv[side, 0:1, :], (128, half)))
        total_there = jnp.transpose(jnp.broadcast_to(st_recv[side, 8:9, :], (128, half)))
        best = jnp.maximum(top_here, top_there)
        here = jnp.exp2((top_here - best) * factor)
        there = jnp.exp2((top_there - best) * factor)
        num = summed[span] * here + po_recv[side].astype(f32) * there
        den = total[span] * here + total_there * there
        fbuf[span, :] = num / den
    for j in range(QPK):
        feature = fbuf[pl.ds(j, NEW, stride=QPK), :]
        gather[c, r, :, j * head_size : (j + 1) * head_size] = feature.astype(bf16)

    def pass_on(at, slot_c, slot_r, peer):
        block = gather.at[slot_c, slot_r]
        copy = pltpu.make_async_remote_copy(
            src_ref=block, dst_ref=block,
            send_sem=g_send.at[at], recv_sem=g_recv.at[at],
            device_id=peer, device_id_type=MESH,
        )
        copy.start()
        return copy

    g_far = pass_on(0, c, r, {"roll": far})
    g_sib = pass_on(1, c, r, {"roll": sib})
    g_ctx = pass_on(2, c, r, partner)
    g_diag = pass_on(3, c, r, {"ctx": other, "roll": far})
    g_far.wait_recv()
    f_far = pass_on(4, c, far, {"roll": sib})
    for at in range(2):
        for cut in range(WCUT):
            local[("w", at, cut)].wait()
    g_sib.wait_recv()
    f_far.wait_recv()

    n_cols = wbuf.shape[2] // COLS
    tokens = gather.shape[1] * NEW

    def project(head, at):
        features = gather[head].reshape(tokens, depth)
        return jnp.dot(
            features, wbuf[head, :, at * COLS : (at + 1) * COLS], preferred_element_type=f32
        )

    f_ctx = f_diag = None
    for at in range(n_cols):
        accbuf[:, at * COLS : (at + 1) * COLS] = project(c, at)
        if at == n_cols // 2 - 1:
            g_ctx.wait_recv()
            f_ctx = pass_on(5, other, r, {"roll": sib})
        if at == n_cols - 2:
            g_diag.wait_recv()
            f_diag = pass_on(6, other, far, {"roll": sib})
    f_ctx.wait_recv()
    f_diag.wait_recv()

    rs_copies = []
    for at in range(n_cols):
        span = slice(at * COLS, (at + 1) * COLS)
        part = accbuf[:, span] + project(other, at)
        accbuf[:, span] = part
        rs_send[:, :, span] = part.astype(bf16).reshape(n_head, NEW, COLS)
        for off in range(n_head - 1, 0, -1):
            to = lax.rem(h + off, n_head)
            copy = pltpu.make_async_remote_copy(
                src_ref=rs_send.at[to, :, span],
                dst_ref=rs_recv.at[off - 1, :, span],
                send_sem=rs_send_sem.at[off - 1, at],
                recv_sem=rs_recv_sem.at[off - 1, at],
                device_id={"head": to},
                device_id_type=MESH,
            )
            copy.start()
            rs_copies.append((at, copy))

    own = pl.ds(pl.multiple_of(h * NEW, NEW), NEW)
    for at in range(n_cols):
        span = slice(at * COLS, (at + 1) * COLS)
        for place, copy in rs_copies:
            if place == at:
                copy.wait_recv()
        value = accbuf[own, span]
        for off in range(n_head - 1):
            value = value + rs_recv[off, :, span].astype(f32)
        out_ref[0, :, span] = value.astype(bf16)

    for copy in q_copies + p_copies + s_copies:
        copy.wait_send()
    for copy in (g_far, g_sib, g_ctx, g_diag, f_far, f_ctx, f_diag):
        copy.wait_send()
    for _, copy in rs_copies:
        copy.wait_send()


def fused_body(n_head, queries, cache_keys, cache_values, new_keys, new_values, lengths, positions, out_weight):
    f32, bf16 = jnp.float32, jnp.bfloat16
    _, heads, slots, head_size = cache_keys.shape
    half = queries.shape[2]
    rows = 2 * half
    width = out_weight.shape[1]
    depth = out_weight.shape[0] // heads
    n_cols = width // COLS
    dma = pltpu.SemaphoreType.DMA
    anywhere = pl.BlockSpec(memory_space=pl.ANY)
    scalars = pl.BlockSpec(memory_space=pltpu.SMEM)
    return pl.pallas_call(
        functools.partial(fused_kernel, n_head),
        out_shape=jax.ShapeDtypeStruct((1, NEW, width), bf16),
        in_specs=[anywhere] * 5 + [scalars] * 2 + [anywhere],
        out_specs=pl.BlockSpec(memory_space=pltpu.VMEM),
        scratch_shapes=[
            pltpu.VMEM((heads, rows, head_size), bf16),
            pltpu.VMEM((heads, slots, head_size), bf16),
            pltpu.VMEM((heads, slots, head_size), bf16),
            pltpu.VMEM((NEW, head_size), bf16),
            pltpu.VMEM((NEW, head_size), bf16),
            pltpu.VMEM((heads, depth, width), bf16),
            pltpu.VMEM((rows, slots), f32),
            pltpu.VMEM((2, half, head_size), bf16),
            pltpu.VMEM((2, half, head_size), bf16),
            pltpu.VMEM((2, 16, half), f32),
            pltpu.VMEM((2, 16, half), f32),
            pltpu.VMEM((rows, head_size), f32),
            pltpu.VMEM((2, 4, NEW, depth), bf16),
            pltpu.VMEM((4 * NEW, width), f32),
            pltpu.VMEM((n_head, NEW, width), bf16),
            pltpu.VMEM((n_head - 1, NEW, width), bf16),
            dma, dma((2,)), dma((2,)), dma((2,)), dma((2, WCUT)),
            dma((2,)), dma((2,)), dma((2,)), dma((2,)), dma((2,)), dma((2,)),
            dma((7,)), dma((7,)),
            dma((n_head - 1, n_cols)), dma((n_head - 1, n_cols)),
        ],
        compiler_params=pltpu.CompilerParams(
            collective_id=0, has_side_effects=True, vmem_limit_bytes=48 * 1024 * 1024
        ),
        cost_estimate=pl.CostEstimate(
            flops=4 * heads * rows * slots * head_size + 2 * 4 * NEW * heads * depth * width,
            bytes_accessed=2 * heads * (2 * slots * head_size + depth * width),
            transcendentals=heads * rows * slots,
        ),
    )(queries, cache_keys, cache_values, new_keys, new_values, lengths, positions, out_weight)


def shifted(value, axis, steps):
    count = lax.axis_size(axis)
    pairs = [(source, (source + steps) % count) for source in range(count)]
    return lax.ppermute(value, axis, pairs)


def ring_body(queries, cache_keys, cache_values, new_keys, new_values, lengths, positions, out_weight):
    here = lax.axis_index("ctx")
    n_ctx = lax.axis_size("ctx")
    slots = cache_keys.shape[2]
    head_size = cache_keys.shape[3]
    local_heads = cache_keys.shape[1]
    scale = 1.0 / head_size**0.5
    keys = cache_keys[0]
    values = cache_values[0]
    fresh_keys = new_keys[0]
    fresh_values = new_values[0]
    pos = positions[0]
    slot_ok = here * slots + jnp.arange(slots) < lengths[0]

    def update(state, block, first_row, use_new):
        top_old, total_old, summed_old = state
        count = block.shape[1]
        scores = jnp.einsum("krd,ksd->krs", block, keys, preferred_element_type=jnp.float32) * scale
        scores = jnp.where(slot_ok[None, None, :], scores, NEG)
        fresh = (
            jnp.einsum("krd,kud->kru", block, fresh_keys, preferred_element_type=jnp.float32)
            * scale
        )
        token = (first_row + jnp.arange(count)) // QPK
        allow = jnp.logical_and(pos[None, :] <= pos[token][:, None], use_new)
        fresh = jnp.where(allow[None], fresh, NEG)
        top = jnp.maximum(top_old, jnp.maximum(jnp.max(scores, axis=2), jnp.max(fresh, axis=2)))
        cache_weights = jnp.where(
            slot_ok[None, None, :], jnp.exp(scores - top[..., None]), 0.0
        ).astype(jnp.bfloat16)
        fresh_weights = jnp.where(allow[None], jnp.exp(fresh - top[..., None]), 0.0).astype(
            jnp.bfloat16
        )
        factor = jnp.exp(top_old - top)
        total = total_old * factor + jnp.sum(cache_weights.astype(jnp.float32), axis=2)
        total = total + jnp.sum(fresh_weights.astype(jnp.float32), axis=2)
        summed = summed_old * factor[..., None]
        summed = summed + jnp.einsum(
            "krs,ksd->krd", cache_weights, values, preferred_element_type=jnp.float32
        )
        summed = summed + jnp.einsum(
            "kru,kud->krd", fresh_weights, fresh_values, preferred_element_type=jnp.float32
        )
        return (top, total, summed)

    block = queries[0]
    block_rows = block.shape[1]
    state = update(
        (
            jnp.full((local_heads, block_rows), NEG, jnp.float32),
            jnp.zeros((local_heads, block_rows), jnp.float32),
            jnp.zeros((local_heads, block_rows, head_size), jnp.float32),
        ),
        block,
        here * block_rows,
        True,
    )

    def turn(step, carry):
        moving, top, total, summed = carry
        moving = shifted(moving, "ctx", 1)
        top, total, summed = shifted((top, total, summed), "ctx", 1)
        top, total, summed = update((top, total, summed), moving, 0, False)
        return (moving, top, total, summed)

    moving, top, total, summed = lax.fori_loop(
        0, n_ctx - 1, turn, (block, state[0], state[1], state[2])
    )
    attended = (summed / total[..., None]).astype(jnp.bfloat16)
    every = lax.all_gather(attended[None], ("ctx", "roll"), axis=0, tiled=True)
    n_roll = every.shape[0] // n_ctx
    every = every.reshape(n_ctx, n_roll, local_heads, block_rows, head_size)
    every = jnp.roll(every, 1, axis=0)
    rows_all = every.transpose(1, 2, 0, 3, 4).reshape(
        n_roll, local_heads, n_ctx * block_rows, head_size
    )
    n_roll = rows_all.shape[0]
    features = rows_all.reshape(n_roll, local_heads, NEW, QPK, head_size).transpose(0, 2, 1, 3, 4)
    features = features.reshape(n_roll, NEW, local_heads * QPK * head_size)
    return lax.psum_scatter(
        jnp.einsum("rtf,fc->rtc", features, out_weight, preferred_element_type=jnp.float32).astype(
            jnp.bfloat16
        ),
        "head",
        scatter_dimension=0,
        tiled=True,
    )


def solution(mesh):
    in_specs = (
        P("roll", "head", "ctx", None),
        P("roll", "head", "ctx", None),
        P("roll", "head", "ctx", None),
        P("roll", "head", None, None),
        P("roll", "head", None, None),
        P("roll"),
        P("roll", None),
        P("head", ("ctx", "roll")),
    )
    out_specs = P("head", None, ("ctx", "roll"))
    body = ring_body
    if (mesh.shape["ctx"], mesh.shape["head"], mesh.shape["roll"]) == (2, 4, 4):
        body = functools.partial(fused_body, mesh.shape["head"])
    return jax.shard_map(body, mesh=mesh, in_specs=in_specs, out_specs=out_specs, check_vma=False)
```

```python
import functools
import math

import jax
import jax.numpy as jnp
from jax import lax
from jax.experimental import pallas as pl
from jax.experimental.pallas import tpu as pltpu
from jax.sharding import PartitionSpec as P

NEW = 16
QPK = 16


NEG = -1e30

MESH = pl.DeviceIdType.MESH
CHUNK = 512
COLS = 512
WCUT = 4


def fused_kernel(
    n_head,
    q_hbm, k_hbm, v_hbm, fk_hbm, fv_hbm, len_ref, pos_ref, w_hbm,
    out_ref,
    qbuf, kbuf, vbuf, fkbuf, fvbuf, wbuf, sbuf,
    po_send, po_recv, st_send, st_recv, fbuf, gather, accbuf, rs_send, rs_recv,
    q_sem, k_sem, v_sem, f_sem, w_sem,
    qx_send, qx_recv, px_send, px_recv, sx_send, sx_recv,
    g_send, g_recv, rs_send_sem, rs_recv_sem,
):
    f32, bf16 = jnp.float32, jnp.bfloat16
    c, h, r = lax.axis_index("ctx"), lax.axis_index("head"), lax.axis_index("roll")
    other = 1 - c
    sib = r + 1 - 2 * lax.rem(r, 2)
    far = lax.rem(r + 2, 4)
    far_sib = lax.rem(sib + 2, 4)
    partner = {"ctx": other}
    rows, head_size = qbuf.shape[1], qbuf.shape[2]
    half = rows // 2
    slots = kbuf.shape[1]
    factor = math.log2(math.e) / math.sqrt(head_size)

    barrier = pltpu.get_barrier_semaphore()
    peers = [partner, {"roll": sib}, {"roll": far}, {"ctx": other, "roll": far}]
    peers += [{"head": lax.rem(h + off, n_head)} for off in range(1, n_head)]
    for peer in peers:
        pl.semaphore_signal(barrier, inc=1, device_id=peer, device_id_type=MESH)

    local = {}

    def fetch(name, src, dst, sem):
        local[name] = pltpu.make_async_copy(src, dst, sem)
        local[name].start()

    mine = pl.ds(pl.multiple_of(c * half, half), half)
    fetch("q", q_hbm.at[0], qbuf.at[:, mine, :], q_sem)
    fetch("k0", k_hbm.at[0, other], kbuf.at[other], k_sem.at[0])
    fetch("v0", v_hbm.at[0, other], vbuf.at[other], v_sem.at[0])
    fetch("k1", k_hbm.at[0, c], kbuf.at[c], k_sem.at[1])
    fetch("v1", v_hbm.at[0, c], vbuf.at[c], v_sem.at[1])
    fetch("fk", fk_hbm.at[0, c], fkbuf, f_sem.at[0])
    fetch("fv", fv_hbm.at[0, c], fvbuf, f_sem.at[1])

    pl.semaphore_wait(barrier, len(peers))

    q_copies = []
    for at, head in enumerate((c, other)):
        q_copies.append(
            pltpu.make_async_remote_copy(
                src_ref=q_hbm.at[0, head],
                dst_ref=qbuf.at[head, mine, :],
                send_sem=qx_send.at[at],
                recv_sem=qx_recv.at[at],
                device_id=partner,
                device_id_type=MESH,
            )
        )
        q_copies[-1].start()

    depth = w_hbm.shape[0] // 2
    piece = depth // WCUT
    for at, head in enumerate((c, other)):
        for cut in range(WCUT):
            fetch(
                ("w", at, cut),
                w_hbm.at[pl.ds(pl.multiple_of(head * depth + cut * piece, piece), piece), :],
                wbuf.at[head, pl.ds(cut * piece, piece), :],
                w_sem.at[at, cut],
            )

    length = len_ref[0]
    first_slot = c * slots

    def scores(query, head):
        fold = jnp.full((query.shape[0], 128), NEG, f32)
        for at in range(slots // CHUNK):
            span = slice(at * CHUNK, (at + 1) * CHUNK)
            part = lax.dot_general(
                query, kbuf[head, span, :], (((1,), (1,)), ((), ())), preferred_element_type=f32
            )
            slot = first_slot + at * CHUNK + lax.broadcasted_iota(jnp.int32, (1, CHUNK), 1)
            part = part + jnp.where(slot < length, 0.0, NEG)
            sbuf[0 : query.shape[0], span] = part
            for lane in range(CHUNK // 128):
                fold = jnp.maximum(fold, part[:, lane * 128 : (lane + 1) * 128])
        return jnp.max(fold, axis=1, keepdims=True)

    def weighted(count, head, top):
        ones = jnp.ones((CHUNK, 128), bf16)
        acc = jnp.zeros((count, head_size + 128), f32)
        for at in range(slots // CHUNK):
            span = slice(at * CHUNK, (at + 1) * CHUNK)
            weights = jnp.exp2((sbuf[0:count, span] - top) * factor).astype(bf16)
            both = jnp.concatenate([vbuf[head, span, :], ones], axis=1)
            acc = acc + jnp.dot(weights, both, preferred_element_type=f32)
        return acc[:, :head_size], acc[:, head_size:]

    lane = lax.broadcasted_iota(jnp.int32, (half, 128), 1)
    p_copies, s_copies = [], []

    def give_back(at, side):
        query = qbuf[other, pl.ds(pl.multiple_of(side * half, half), half), :]
        top = scores(query, other)
        if at == 0:
            local["v0"].wait()
        summed, total = weighted(half, other, top)
        po_send[side] = summed.astype(bf16)
        turned = jnp.transpose(jnp.where(lane < 64, jnp.broadcast_to(top, (half, 128)), total))
        st_send[side, 0:8, :] = turned[0:8, :]
        st_send[side, 8:16, :] = turned[64:72, :]
        p_copies.append(
            pltpu.make_async_remote_copy(
                src_ref=po_send.at[side], dst_ref=po_recv.at[side],
                send_sem=px_send.at[at], recv_sem=px_recv.at[at],
                device_id=partner, device_id_type=MESH,
            )
        )
        s_copies.append(
            pltpu.make_async_remote_copy(
                src_ref=st_send.at[side], dst_ref=st_recv.at[side],
                send_sem=sx_send.at[at], recv_sem=sx_recv.at[at],
                device_id=partner, device_id_type=MESH,
            )
        )
        s_copies[-1].start()
        p_copies[-1].start()

    token_here = lax.broadcasted_iota(jnp.int32, (half, NEW), 0) // QPK
    fresh_at = lax.broadcasted_iota(jnp.int32, (half, NEW), 1)

    def keep(at, side):
        token = token_here + side * (half // QPK)
        row_pos = jnp.zeros((half, NEW), jnp.int32)
        new_pos = jnp.zeros((half, NEW), jnp.int32)
        for t in range(NEW):
            value = pos_ref[0, t]
            row_pos = jnp.where(token == t, value, row_pos)
            new_pos = jnp.where(fresh_at == t, value, new_pos)
        allow = new_pos <= row_pos
        query = qbuf[c, pl.ds(pl.multiple_of(side * half, half), half), :]
        top = scores(query, c)
        fresh = lax.dot_general(
            query, fkbuf[...], (((1,), (1,)), ((), ())), preferred_element_type=f32
        )
        fresh = jnp.where(allow, fresh, NEG)
        top = jnp.maximum(top, jnp.max(fresh, axis=1, keepdims=True))
        if at == 0:
            local["v1"].wait()
            local["fv"].wait()
        summed, total = weighted(half, c, top)
        fresh_weights = jnp.where(allow, jnp.exp2((fresh - top) * factor), 0.0).astype(bf16)
        summed = summed + jnp.dot(fresh_weights, fvbuf[...], preferred_element_type=f32)
        total = total + jnp.sum(fresh_weights.astype(f32), axis=1, keepdims=True)
        return jnp.broadcast_to(top, (half, 128)), total, summed

    def merge(side, state):
        top_here, total, summed = state
        top_there = jnp.transpose(jnp.broadcast_to(st_recv[side, 0:1, :], (128, half)))
        total_there = jnp.transpose(jnp.broadcast_to(st_recv[side, 8:9, :], (128, half)))
        best = jnp.maximum(top_here, top_there)
        here = jnp.exp2((top_here - best) * factor)
        there = jnp.exp2((top_there - best) * factor)
        num = summed * here + po_recv[side].astype(f32) * there
        den = total * here + total_there * there
        fbuf[pl.ds(pl.multiple_of(side * half, half), half), :] = num / den

    local["q"].wait()
    local["k0"].wait()
    give_back(0, c)
    local["k1"].wait()
    local["fk"].wait()
    state_mine = keep(0, c)
    q_copies[0].wait_recv()
    give_back(1, other)
    q_copies[1].wait_recv()
    state_other = keep(1, other)

    s_copies[0].wait_recv()
    p_copies[0].wait_recv()
    merge(other, state_other)
    s_copies[1].wait_recv()
    p_copies[1].wait_recv()
    merge(c, state_mine)
    for j in range(QPK):
        feature = fbuf[pl.ds(j, NEW, stride=QPK), :]
        gather[c, r, :, j * head_size : (j + 1) * head_size] = feature.astype(bf16)

    def pass_on(at, slot_c, slot_r, peer):
        block = gather.at[slot_c, slot_r]
        copy = pltpu.make_async_remote_copy(
            src_ref=block, dst_ref=block,
            send_sem=g_send.at[at], recv_sem=g_recv.at[at],
            device_id=peer, device_id_type=MESH,
        )
        copy.start()
        return copy

    g_far = pass_on(0, c, r, {"roll": far})
    g_sib = pass_on(1, c, r, {"roll": sib})
    g_ctx = pass_on(2, c, r, partner)
    g_diag = pass_on(3, c, r, {"ctx": other, "roll": far})
    g_far.wait_recv()
    f_far = pass_on(4, c, far, {"roll": sib})
    for at in range(2):
        for cut in range(WCUT):
            local[("w", at, cut)].wait()
    g_sib.wait_recv()
    f_far.wait_recv()

    n_cols = wbuf.shape[2] // COLS
    tokens = gather.shape[1] * NEW

    def project(head, at):
        features = gather[head].reshape(tokens, depth)
        return jnp.dot(
            features, wbuf[head, :, at * COLS : (at + 1) * COLS], preferred_element_type=f32
        )

    f_ctx = f_diag = None
    for at in range(n_cols):
        accbuf[:, at * COLS : (at + 1) * COLS] = project(c, at)
        if at == n_cols // 2 - 1:
            g_ctx.wait_recv()
            f_ctx = pass_on(5, other, r, {"roll": sib})
        if at == n_cols - 2:
            g_diag.wait_recv()
            f_diag = pass_on(6, other, far, {"roll": sib})
    f_ctx.wait_recv()
    f_diag.wait_recv()

    rs_copies = []
    for at in range(n_cols):
        span = slice(at * COLS, (at + 1) * COLS)
        part = accbuf[:, span] + project(other, at)
        accbuf[:, span] = part
        rs_send[:, :, span] = part.astype(bf16).reshape(n_head, NEW, COLS)
        for off in range(n_head - 1, 0, -1):
            to = lax.rem(h + off, n_head)
            copy = pltpu.make_async_remote_copy(
                src_ref=rs_send.at[to, :, span],
                dst_ref=rs_recv.at[off - 1, :, span],
                send_sem=rs_send_sem.at[off - 1, at],
                recv_sem=rs_recv_sem.at[off - 1, at],
                device_id={"head": to},
                device_id_type=MESH,
            )
            copy.start()
            rs_copies.append((at, copy))

    own = pl.ds(pl.multiple_of(h * NEW, NEW), NEW)
    for at in range(n_cols):
        span = slice(at * COLS, (at + 1) * COLS)
        for place, copy in rs_copies:
            if place == at:
                copy.wait_recv()
        value = accbuf[own, span]
        for off in range(n_head - 1):
            value = value + rs_recv[off, :, span].astype(f32)
        out_ref[0, :, span] = value.astype(bf16)

    for copy in q_copies + p_copies + s_copies:
        copy.wait_send()
    for copy in (g_far, g_sib, g_ctx, g_diag, f_far, f_ctx, f_diag):
        copy.wait_send()
    for _, copy in rs_copies:
        copy.wait_send()


def fused_body(n_head, queries, cache_keys, cache_values, new_keys, new_values, lengths, positions, out_weight):
    f32, bf16 = jnp.float32, jnp.bfloat16
    _, heads, slots, head_size = cache_keys.shape
    half = queries.shape[2]
    rows = 2 * half
    width = out_weight.shape[1]
    depth = out_weight.shape[0] // heads
    n_cols = width // COLS
    dma = pltpu.SemaphoreType.DMA
    pinned = [
        pltpu.with_memory_space_constraint(array, pltpu.HBM)
        for array in (queries, cache_keys, cache_values, new_keys, new_values, positions)
    ]
    anywhere = pl.BlockSpec(memory_space=pltpu.HBM)
    scalars = pl.BlockSpec(memory_space=pltpu.SMEM)
    return pl.pallas_call(
        functools.partial(fused_kernel, n_head),
        out_shape=jax.ShapeDtypeStruct((1, NEW, width), bf16),
        in_specs=[anywhere] * 5 + [scalars] * 2 + [anywhere],
        out_specs=pl.BlockSpec(memory_space=pltpu.VMEM),
        scratch_shapes=[
            pltpu.VMEM((heads, rows, head_size), bf16),
            pltpu.VMEM((heads, slots, head_size), bf16),
            pltpu.VMEM((heads, slots, head_size), bf16),
            pltpu.VMEM((NEW, head_size), bf16),
            pltpu.VMEM((NEW, head_size), bf16),
            pltpu.VMEM((heads, depth, width), bf16),
            pltpu.VMEM((half, slots), f32),
            pltpu.VMEM((2, half, head_size), bf16),
            pltpu.VMEM((2, half, head_size), bf16),
            pltpu.VMEM((2, 16, half), f32),
            pltpu.VMEM((2, 16, half), f32),
            pltpu.VMEM((rows, head_size), f32),
            pltpu.VMEM((2, 4, NEW, depth), bf16),
            pltpu.VMEM((4 * NEW, width), f32),
            pltpu.VMEM((n_head, NEW, width), bf16),
            pltpu.VMEM((n_head - 1, NEW, width), bf16),
            dma, dma((2,)), dma((2,)), dma((2,)), dma((2, WCUT)),
            dma((2,)), dma((2,)), dma((2,)), dma((2,)), dma((2,)), dma((2,)),
            dma((7,)), dma((7,)),
            dma((n_head - 1, n_cols)), dma((n_head - 1, n_cols)),
        ],
        compiler_params=pltpu.CompilerParams(
            collective_id=0, has_side_effects=True, vmem_limit_bytes=48 * 1024 * 1024
        ),
        cost_estimate=pl.CostEstimate(
            flops=4 * heads * rows * slots * head_size + 2 * 4 * NEW * heads * depth * width,
            bytes_accessed=2 * heads * (2 * slots * head_size + depth * width),
            transcendentals=heads * rows * slots,
        ),
    )(*pinned[:5], lengths, pinned[5], out_weight)


def shifted(value, axis, steps):
    count = lax.axis_size(axis)
    pairs = [(source, (source + steps) % count) for source in range(count)]
    return lax.ppermute(value, axis, pairs)


def ring_body(queries, cache_keys, cache_values, new_keys, new_values, lengths, positions, out_weight):
    here = lax.axis_index("ctx")
    n_ctx = lax.axis_size("ctx")
    slots = cache_keys.shape[2]
    head_size = cache_keys.shape[3]
    local_heads = cache_keys.shape[1]
    scale = 1.0 / head_size**0.5
    keys = cache_keys[0]
    values = cache_values[0]
    fresh_keys = new_keys[0]
    fresh_values = new_values[0]
    pos = positions[0]
    slot_ok = here * slots + jnp.arange(slots) < lengths[0]

    def update(state, block, first_row, use_new):
        top_old, total_old, summed_old = state
        count = block.shape[1]
        scores = jnp.einsum("krd,ksd->krs", block, keys, preferred_element_type=jnp.float32) * scale
        scores = jnp.where(slot_ok[None, None, :], scores, NEG)
        fresh = (
            jnp.einsum("krd,kud->kru", block, fresh_keys, preferred_element_type=jnp.float32)
            * scale
        )
        token = (first_row + jnp.arange(count)) // QPK
        allow = jnp.logical_and(pos[None, :] <= pos[token][:, None], use_new)
        fresh = jnp.where(allow[None], fresh, NEG)
        top = jnp.maximum(top_old, jnp.maximum(jnp.max(scores, axis=2), jnp.max(fresh, axis=2)))
        cache_weights = jnp.where(
            slot_ok[None, None, :], jnp.exp(scores - top[..., None]), 0.0
        ).astype(jnp.bfloat16)
        fresh_weights = jnp.where(allow[None], jnp.exp(fresh - top[..., None]), 0.0).astype(
            jnp.bfloat16
        )
        factor = jnp.exp(top_old - top)
        total = total_old * factor + jnp.sum(cache_weights.astype(jnp.float32), axis=2)
        total = total + jnp.sum(fresh_weights.astype(jnp.float32), axis=2)
        summed = summed_old * factor[..., None]
        summed = summed + jnp.einsum(
            "krs,ksd->krd", cache_weights, values, preferred_element_type=jnp.float32
        )
        summed = summed + jnp.einsum(
            "kru,kud->krd", fresh_weights, fresh_values, preferred_element_type=jnp.float32
        )
        return (top, total, summed)

    block = queries[0]
    block_rows = block.shape[1]
    state = update(
        (
            jnp.full((local_heads, block_rows), NEG, jnp.float32),
            jnp.zeros((local_heads, block_rows), jnp.float32),
            jnp.zeros((local_heads, block_rows, head_size), jnp.float32),
        ),
        block,
        here * block_rows,
        True,
    )

    def turn(step, carry):
        moving, top, total, summed = carry
        moving = shifted(moving, "ctx", 1)
        top, total, summed = shifted((top, total, summed), "ctx", 1)
        top, total, summed = update((top, total, summed), moving, 0, False)
        return (moving, top, total, summed)

    moving, top, total, summed = lax.fori_loop(
        0, n_ctx - 1, turn, (block, state[0], state[1], state[2])
    )
    attended = (summed / total[..., None]).astype(jnp.bfloat16)
    every = lax.all_gather(attended[None], ("ctx", "roll"), axis=0, tiled=True)
    n_roll = every.shape[0] // n_ctx
    every = every.reshape(n_ctx, n_roll, local_heads, block_rows, head_size)
    every = jnp.roll(every, 1, axis=0)
    rows_all = every.transpose(1, 2, 0, 3, 4).reshape(
        n_roll, local_heads, n_ctx * block_rows, head_size
    )
    n_roll = rows_all.shape[0]
    features = rows_all.reshape(n_roll, local_heads, NEW, QPK, head_size).transpose(0, 2, 1, 3, 4)
    features = features.reshape(n_roll, NEW, local_heads * QPK * head_size)
    return lax.psum_scatter(
        jnp.einsum("rtf,fc->rtc", features, out_weight, preferred_element_type=jnp.float32).astype(
            jnp.bfloat16
        ),
        "head",
        scatter_dimension=0,
        tiled=True,
    )


def solution(mesh):
    in_specs = (
        P("roll", "head", "ctx", None),
        P("roll", "head", "ctx", None),
        P("roll", "head", "ctx", None),
        P("roll", "head", None, None),
        P("roll", "head", None, None),
        P("roll"),
        P("roll", None),
        P("head", ("ctx", "roll")),
    )
    out_specs = P("head", None, ("ctx", "roll"))
    body = ring_body
    if (mesh.shape["ctx"], mesh.shape["head"], mesh.shape["roll"]) == (2, 4, 4):
        body = functools.partial(fused_body, mesh.shape["head"])
    return jax.shard_map(body, mesh=mesh, in_specs=in_specs, out_specs=out_specs, check_vma=False)
```

```python
import functools
import math

import jax
import jax.numpy as jnp
from jax import lax
from jax.experimental import pallas as pl
from jax.experimental.pallas import tpu as pltpu
from jax.sharding import PartitionSpec as P

NEW = 16
QPK = 16


NEG = -1e30

MESH = pl.DeviceIdType.MESH
CHUNK = 512
COLS = 512
WCUT = 4


def fused_kernel(
    n_head,
    q_hbm, k_hbm, v_hbm, fk_hbm, fv_hbm, len_ref, pos_hbm, w_hbm,
    out_ref,
    pos_ref, qbuf, kbuf, vbuf, fkbuf, fvbuf, wbuf, sbuf,
    po_send, po_recv, st_send, st_recv, fbuf, gather, accbuf, rs_send, rs_recv,
    q_sem, k_sem, v_sem, f_sem, n_sem, w_sem,
    qx_send, qx_recv, px_send, px_recv, sx_send, sx_recv,
    g_send, g_recv, rs_send_sem, rs_recv_sem,
):
    f32, bf16 = jnp.float32, jnp.bfloat16
    c, h, r = lax.axis_index("ctx"), lax.axis_index("head"), lax.axis_index("roll")
    other = 1 - c
    sib = r + 1 - 2 * lax.rem(r, 2)
    far = lax.rem(r + 2, 4)
    far_sib = lax.rem(sib + 2, 4)
    partner = {"ctx": other}
    rows, head_size = qbuf.shape[1], qbuf.shape[2]
    half = rows // 2
    slots = kbuf.shape[1]
    factor = math.log2(math.e) / math.sqrt(head_size)

    barrier = pltpu.get_barrier_semaphore()
    peers = [partner, {"roll": sib}, {"roll": far}, {"ctx": other, "roll": far}]
    peers += [{"head": lax.rem(h + off, n_head)} for off in range(1, n_head)]
    for peer in peers:
        pl.semaphore_signal(barrier, inc=1, device_id=peer, device_id_type=MESH)

    local = {}

    def fetch(name, src, dst, sem):
        local[name] = pltpu.make_async_copy(src, dst, sem)
        local[name].start()

    mine = pl.ds(pl.multiple_of(c * half, half), half)
    fetch("q", q_hbm.at[0], qbuf.at[:, mine, :], q_sem)
    fetch("k0", k_hbm.at[0, other], kbuf.at[other], k_sem.at[0])
    fetch("v0", v_hbm.at[0, other], vbuf.at[other], v_sem.at[0])
    fetch("pos", pos_hbm, pos_ref, n_sem)
    fetch("k1", k_hbm.at[0, c], kbuf.at[c], k_sem.at[1])
    fetch("v1", v_hbm.at[0, c], vbuf.at[c], v_sem.at[1])
    fetch("fk", fk_hbm.at[0, c], fkbuf, f_sem.at[0])
    fetch("fv", fv_hbm.at[0, c], fvbuf, f_sem.at[1])

    pl.semaphore_wait(barrier, len(peers))

    q_copies = []
    for at, head in enumerate((c, other)):
        q_copies.append(
            pltpu.make_async_remote_copy(
                src_ref=q_hbm.at[0, head],
                dst_ref=qbuf.at[head, mine, :],
                send_sem=qx_send.at[at],
                recv_sem=qx_recv.at[at],
                device_id=partner,
                device_id_type=MESH,
            )
        )
        q_copies[-1].start()

    depth = w_hbm.shape[0] // 2
    piece = depth // WCUT
    for at, head in enumerate((c, other)):
        for cut in range(WCUT):
            fetch(
                ("w", at, cut),
                w_hbm.at[pl.ds(pl.multiple_of(head * depth + cut * piece, piece), piece), :],
                wbuf.at[head, pl.ds(cut * piece, piece), :],
                w_sem.at[at, cut],
            )

    local["pos"].wait()
    length = len_ref[0]
    first_slot = c * slots

    def scores(query, head):
        fold = jnp.full((query.shape[0], 128), NEG, f32)
        for at in range(slots // CHUNK):
            span = slice(at * CHUNK, (at + 1) * CHUNK)
            part = lax.dot_general(
                query, kbuf[head, span, :], (((1,), (1,)), ((), ())), preferred_element_type=f32
            )
            slot = first_slot + at * CHUNK + lax.broadcasted_iota(jnp.int32, (1, CHUNK), 1)
            part = part + jnp.where(slot < length, 0.0, NEG)
            sbuf[0 : query.shape[0], span] = part
            for lane in range(CHUNK // 128):
                fold = jnp.maximum(fold, part[:, lane * 128 : (lane + 1) * 128])
        return jnp.max(fold, axis=1, keepdims=True)

    def weighted(count, head, top):
        ones = jnp.ones((CHUNK, 128), bf16)
        acc = jnp.zeros((count, head_size + 128), f32)
        for at in range(slots // CHUNK):
            span = slice(at * CHUNK, (at + 1) * CHUNK)
            weights = jnp.exp2((sbuf[0:count, span] - top) * factor).astype(bf16)
            both = jnp.concatenate([vbuf[head, span, :], ones], axis=1)
            acc = acc + jnp.dot(weights, both, preferred_element_type=f32)
        return acc[:, :head_size], acc[:, head_size:]

    lane = lax.broadcasted_iota(jnp.int32, (half, 128), 1)
    p_copies, s_copies = [], []

    def give_back(at, side):
        query = qbuf[other, pl.ds(pl.multiple_of(side * half, half), half), :]
        top = scores(query, other)
        if at == 0:
            local["v0"].wait()
        summed, total = weighted(half, other, top)
        po_send[side] = summed.astype(bf16)
        turned = jnp.transpose(jnp.where(lane < 64, jnp.broadcast_to(top, (half, 128)), total))
        st_send[side, 0:8, :] = turned[0:8, :]
        st_send[side, 8:16, :] = turned[64:72, :]
        p_copies.append(
            pltpu.make_async_remote_copy(
                src_ref=po_send.at[side], dst_ref=po_recv.at[side],
                send_sem=px_send.at[at], recv_sem=px_recv.at[at],
                device_id=partner, device_id_type=MESH,
            )
        )
        s_copies.append(
            pltpu.make_async_remote_copy(
                src_ref=st_send.at[side], dst_ref=st_recv.at[side],
                send_sem=sx_send.at[at], recv_sem=sx_recv.at[at],
                device_id=partner, device_id_type=MESH,
            )
        )
        s_copies[-1].start()
        p_copies[-1].start()

    token_here = lax.broadcasted_iota(jnp.int32, (half, NEW), 0) // QPK
    fresh_at = lax.broadcasted_iota(jnp.int32, (half, NEW), 1)

    def keep(at, side):
        token = token_here + side * (half // QPK)
        row_pos = jnp.zeros((half, NEW), jnp.int32)
        new_pos = jnp.zeros((half, NEW), jnp.int32)
        for t in range(NEW):
            value = pos_ref[0, t]
            row_pos = jnp.where(token == t, value, row_pos)
            new_pos = jnp.where(fresh_at == t, value, new_pos)
        allow = new_pos <= row_pos
        query = qbuf[c, pl.ds(pl.multiple_of(side * half, half), half), :]
        top = scores(query, c)
        fresh = lax.dot_general(
            query, fkbuf[...], (((1,), (1,)), ((), ())), preferred_element_type=f32
        )
        fresh = jnp.where(allow, fresh, NEG)
        top = jnp.maximum(top, jnp.max(fresh, axis=1, keepdims=True))
        if at == 0:
            local["v1"].wait()
            local["fv"].wait()
        summed, total = weighted(half, c, top)
        fresh_weights = jnp.where(allow, jnp.exp2((fresh - top) * factor), 0.0).astype(bf16)
        summed = summed + jnp.dot(fresh_weights, fvbuf[...], preferred_element_type=f32)
        total = total + jnp.sum(fresh_weights.astype(f32), axis=1, keepdims=True)
        return jnp.broadcast_to(top, (half, 128)), total, summed

    def merge(side, state):
        top_here, total, summed = state
        top_there = jnp.transpose(jnp.broadcast_to(st_recv[side, 0:1, :], (128, half)))
        total_there = jnp.transpose(jnp.broadcast_to(st_recv[side, 8:9, :], (128, half)))
        best = jnp.maximum(top_here, top_there)
        here = jnp.exp2((top_here - best) * factor)
        there = jnp.exp2((top_there - best) * factor)
        num = summed * here + po_recv[side].astype(f32) * there
        den = total * here + total_there * there
        fbuf[pl.ds(pl.multiple_of(side * half, half), half), :] = num / den

    local["q"].wait()
    local["k0"].wait()
    give_back(0, c)
    local["k1"].wait()
    local["fk"].wait()
    state_mine = keep(0, c)
    q_copies[0].wait_recv()
    give_back(1, other)
    q_copies[1].wait_recv()
    state_other = keep(1, other)

    s_copies[0].wait_recv()
    p_copies[0].wait_recv()
    merge(other, state_other)
    s_copies[1].wait_recv()
    p_copies[1].wait_recv()
    merge(c, state_mine)
    for j in range(QPK):
        feature = fbuf[pl.ds(j, NEW, stride=QPK), :]
        gather[c, r, :, j * head_size : (j + 1) * head_size] = feature.astype(bf16)

    def pass_on(at, slot_c, slot_r, peer):
        block = gather.at[slot_c, slot_r]
        copy = pltpu.make_async_remote_copy(
            src_ref=block, dst_ref=block,
            send_sem=g_send.at[at], recv_sem=g_recv.at[at],
            device_id=peer, device_id_type=MESH,
        )
        copy.start()
        return copy

    g_far = pass_on(0, c, r, {"roll": far})
    g_sib = pass_on(1, c, r, {"roll": sib})
    g_ctx = pass_on(2, c, r, partner)
    g_diag = pass_on(3, c, r, {"ctx": other, "roll": far})
    g_far.wait_recv()
    f_far = pass_on(4, c, far, {"roll": sib})
    g_ctx.wait_recv()
    f_ctx = pass_on(5, other, r, {"roll": sib})
    for at in range(2):
        for cut in range(WCUT):
            local[("w", at, cut)].wait()
    g_sib.wait_recv()
    f_far.wait_recv()

    n_cols = wbuf.shape[2] // COLS
    tokens = gather.shape[1] * NEW

    def project(head, at):
        features = gather[head].reshape(tokens, depth)
        return jnp.dot(
            features, wbuf[head, :, at * COLS : (at + 1) * COLS], preferred_element_type=f32
        )

    f_diag = None
    for at in range(n_cols):
        accbuf[:, at * COLS : (at + 1) * COLS] = project(c, at)
        if at == n_cols // 2 - 1:
            g_diag.wait_recv()
            f_diag = pass_on(6, other, far, {"roll": sib})
    f_ctx.wait_recv()
    f_diag.wait_recv()

    rs_copies = []
    for at in range(n_cols):
        span = slice(at * COLS, (at + 1) * COLS)
        part = accbuf[:, span] + project(other, at)
        accbuf[:, span] = part
        rs_send[:, :, span] = part.astype(bf16).reshape(n_head, NEW, COLS)
        for off in range(n_head - 1, 0, -1):
            to = lax.rem(h + off, n_head)
            copy = pltpu.make_async_remote_copy(
                src_ref=rs_send.at[to, :, span],
                dst_ref=rs_recv.at[off - 1, :, span],
                send_sem=rs_send_sem.at[off - 1, at],
                recv_sem=rs_recv_sem.at[off - 1, at],
                device_id={"head": to},
                device_id_type=MESH,
            )
            copy.start()
            rs_copies.append((at, copy))

    own = pl.ds(pl.multiple_of(h * NEW, NEW), NEW)
    for at in range(n_cols):
        span = slice(at * COLS, (at + 1) * COLS)
        for place, copy in rs_copies:
            if place == at:
                copy.wait_recv()
        value = accbuf[own, span]
        for off in range(n_head - 1):
            value = value + rs_recv[off, :, span].astype(f32)
        out_ref[0, :, span] = value.astype(bf16)

    for copy in q_copies + p_copies + s_copies:
        copy.wait_send()
    for copy in (g_far, g_sib, g_ctx, g_diag, f_far, f_ctx, f_diag):
        copy.wait_send()
    for _, copy in rs_copies:
        copy.wait_send()


def fused_body(n_head, queries, cache_keys, cache_values, new_keys, new_values, lengths, positions, out_weight):
    f32, bf16 = jnp.float32, jnp.bfloat16
    _, heads, slots, head_size = cache_keys.shape
    half = queries.shape[2]
    rows = 2 * half
    width = out_weight.shape[1]
    depth = out_weight.shape[0] // heads
    n_cols = width // COLS
    dma = pltpu.SemaphoreType.DMA
    pinned = [
        pltpu.with_memory_space_constraint(array, pltpu.HBM)
        for array in (queries, cache_keys, cache_values, new_keys, new_values, positions)
    ]
    anywhere = pl.BlockSpec(memory_space=pltpu.HBM)
    return pl.pallas_call(
        functools.partial(fused_kernel, n_head),
        out_shape=jax.ShapeDtypeStruct((1, NEW, width), bf16),
        in_specs=[anywhere] * 5 + [pl.BlockSpec(memory_space=pltpu.SMEM)] + [anywhere] * 2,
        out_specs=pl.BlockSpec(memory_space=pltpu.VMEM),
        scratch_shapes=[
            pltpu.SMEM(positions.shape, positions.dtype),
            pltpu.VMEM((heads, rows, head_size), bf16),
            pltpu.VMEM((heads, slots, head_size), bf16),
            pltpu.VMEM((heads, slots, head_size), bf16),
            pltpu.VMEM((NEW, head_size), bf16),
            pltpu.VMEM((NEW, head_size), bf16),
            pltpu.VMEM((heads, depth, width), bf16),
            pltpu.VMEM((half, slots), f32),
            pltpu.VMEM((2, half, head_size), bf16),
            pltpu.VMEM((2, half, head_size), bf16),
            pltpu.VMEM((2, 16, half), f32),
            pltpu.VMEM((2, 16, half), f32),
            pltpu.VMEM((rows, head_size), f32),
            pltpu.VMEM((2, 4, NEW, depth), bf16),
            pltpu.VMEM((4 * NEW, width), f32),
            pltpu.VMEM((n_head, NEW, width), bf16),
            pltpu.VMEM((n_head - 1, NEW, width), bf16),
            dma, dma((2,)), dma((2,)), dma((2,)), dma, dma((2, WCUT)),
            dma((2,)), dma((2,)), dma((2,)), dma((2,)), dma((2,)), dma((2,)),
            dma((7,)), dma((7,)),
            dma((n_head - 1, n_cols)), dma((n_head - 1, n_cols)),
        ],
        compiler_params=pltpu.CompilerParams(
            collective_id=0, has_side_effects=True, vmem_limit_bytes=48 * 1024 * 1024
        ),
        cost_estimate=pl.CostEstimate(
            flops=4 * heads * rows * slots * head_size + 2 * 4 * NEW * heads * depth * width,
            bytes_accessed=2 * heads * (2 * slots * head_size + depth * width),
            transcendentals=heads * rows * slots,
        ),
    )(*pinned[:5], lengths, pinned[5], out_weight)


def shifted(value, axis, steps):
    count = lax.axis_size(axis)
    pairs = [(source, (source + steps) % count) for source in range(count)]
    return lax.ppermute(value, axis, pairs)


def ring_body(queries, cache_keys, cache_values, new_keys, new_values, lengths, positions, out_weight):
    here = lax.axis_index("ctx")
    n_ctx = lax.axis_size("ctx")
    slots = cache_keys.shape[2]
    head_size = cache_keys.shape[3]
    local_heads = cache_keys.shape[1]
    scale = 1.0 / head_size**0.5
    keys = cache_keys[0]
    values = cache_values[0]
    fresh_keys = new_keys[0]
    fresh_values = new_values[0]
    pos = positions[0]
    slot_ok = here * slots + jnp.arange(slots) < lengths[0]

    def update(state, block, first_row, use_new):
        top_old, total_old, summed_old = state
        count = block.shape[1]
        scores = jnp.einsum("krd,ksd->krs", block, keys, preferred_element_type=jnp.float32) * scale
        scores = jnp.where(slot_ok[None, None, :], scores, NEG)
        fresh = (
            jnp.einsum("krd,kud->kru", block, fresh_keys, preferred_element_type=jnp.float32)
            * scale
        )
        token = (first_row + jnp.arange(count)) // QPK
        allow = jnp.logical_and(pos[None, :] <= pos[token][:, None], use_new)
        fresh = jnp.where(allow[None], fresh, NEG)
        top = jnp.maximum(top_old, jnp.maximum(jnp.max(scores, axis=2), jnp.max(fresh, axis=2)))
        cache_weights = jnp.where(
            slot_ok[None, None, :], jnp.exp(scores - top[..., None]), 0.0
        ).astype(jnp.bfloat16)
        fresh_weights = jnp.where(allow[None], jnp.exp(fresh - top[..., None]), 0.0).astype(
            jnp.bfloat16
        )
        factor = jnp.exp(top_old - top)
        total = total_old * factor + jnp.sum(cache_weights.astype(jnp.float32), axis=2)
        total = total + jnp.sum(fresh_weights.astype(jnp.float32), axis=2)
        summed = summed_old * factor[..., None]
        summed = summed + jnp.einsum(
            "krs,ksd->krd", cache_weights, values, preferred_element_type=jnp.float32
        )
        summed = summed + jnp.einsum(
            "kru,kud->krd", fresh_weights, fresh_values, preferred_element_type=jnp.float32
        )
        return (top, total, summed)

    block = queries[0]
    block_rows = block.shape[1]
    state = update(
        (
            jnp.full((local_heads, block_rows), NEG, jnp.float32),
            jnp.zeros((local_heads, block_rows), jnp.float32),
            jnp.zeros((local_heads, block_rows, head_size), jnp.float32),
        ),
        block,
        here * block_rows,
        True,
    )

    def turn(step, carry):
        moving, top, total, summed = carry
        moving = shifted(moving, "ctx", 1)
        top, total, summed = shifted((top, total, summed), "ctx", 1)
        top, total, summed = update((top, total, summed), moving, 0, False)
        return (moving, top, total, summed)

    moving, top, total, summed = lax.fori_loop(
        0, n_ctx - 1, turn, (block, state[0], state[1], state[2])
    )
    attended = (summed / total[..., None]).astype(jnp.bfloat16)
    every = lax.all_gather(attended[None], ("ctx", "roll"), axis=0, tiled=True)
    n_roll = every.shape[0] // n_ctx
    every = every.reshape(n_ctx, n_roll, local_heads, block_rows, head_size)
    every = jnp.roll(every, 1, axis=0)
    rows_all = every.transpose(1, 2, 0, 3, 4).reshape(
        n_roll, local_heads, n_ctx * block_rows, head_size
    )
    n_roll = rows_all.shape[0]
    features = rows_all.reshape(n_roll, local_heads, NEW, QPK, head_size).transpose(0, 2, 1, 3, 4)
    features = features.reshape(n_roll, NEW, local_heads * QPK * head_size)
    return lax.psum_scatter(
        jnp.einsum("rtf,fc->rtc", features, out_weight, preferred_element_type=jnp.float32).astype(
            jnp.bfloat16
        ),
        "head",
        scatter_dimension=0,
        tiled=True,
    )


def solution(mesh):
    in_specs = (
        P("roll", "head", "ctx", None),
        P("roll", "head", "ctx", None),
        P("roll", "head", "ctx", None),
        P("roll", "head", None, None),
        P("roll", "head", None, None),
        P("roll"),
        P("roll", None),
        P("head", ("ctx", "roll")),
    )
    out_specs = P("head", None, ("ctx", "roll"))
    body = ring_body
    if (mesh.shape["ctx"], mesh.shape["head"], mesh.shape["roll"]) == (2, 4, 4):
        body = functools.partial(fused_body, mesh.shape["head"])
    return jax.shard_map(body, mesh=mesh, in_specs=in_specs, out_specs=out_specs, check_vma=False)
```

```python
import functools
import math

import jax
import jax.numpy as jnp
from jax import lax
from jax.experimental import pallas as pl
from jax.experimental.pallas import tpu as pltpu
from jax.sharding import PartitionSpec as P

NEW = 16
QPK = 16


NEG = -1e30

MESH = pl.DeviceIdType.MESH
CHUNK = 512
COLS = 512
WCUT = 4


def fused_kernel(
    n_head,
    q_hbm, k_hbm, v_hbm, fk_hbm, fv_hbm, len_ref, pos_hbm, w_hbm,
    out_ref,
    pos_ref, qbuf, kbuf, vbuf, fkbuf, fvbuf, wbuf, sbuf,
    po_send, po_recv, st_send, st_recv, fbuf, gather, accbuf, rs_send, rs_recv,
    q_sem, k_sem, v_sem, f_sem, n_sem, w_sem,
    qx_send, qx_recv, px_send, px_recv, sx_send, sx_recv,
    g_send, g_recv, rs_send_sem, rs_recv_sem,
):
    f32, bf16 = jnp.float32, jnp.bfloat16
    c, h, r = lax.axis_index("ctx"), lax.axis_index("head"), lax.axis_index("roll")
    other = 1 - c
    sib = r + 1 - 2 * lax.rem(r, 2)
    far = lax.rem(r + 2, 4)
    far_sib = lax.rem(sib + 2, 4)
    partner = {"ctx": other}
    rows, head_size = qbuf.shape[1], qbuf.shape[2]
    half = rows // 2
    slots = kbuf.shape[1]
    factor = math.log2(math.e) / math.sqrt(head_size)

    barrier = pltpu.get_barrier_semaphore()
    peers = [partner, {"roll": sib}, {"roll": far}, {"ctx": other, "roll": far}]
    peers += [{"head": lax.rem(h + off, n_head)} for off in range(1, n_head)]
    for peer in peers:
        pl.semaphore_signal(barrier, inc=1, device_id=peer, device_id_type=MESH)

    local = {}

    def fetch(name, src, dst, sem):
        local[name] = pltpu.make_async_copy(src, dst, sem)
        local[name].start()

    mine = pl.ds(pl.multiple_of(c * half, half), half)
    fetch("q", q_hbm.at[0], qbuf.at[:, mine, :], q_sem)
    fetch("k0", k_hbm.at[0, other], kbuf.at[other], k_sem.at[0])
    fetch("v0", v_hbm.at[0, other], vbuf.at[other], v_sem.at[0])
    fetch("pos", pos_hbm, pos_ref, n_sem)
    fetch("k1", k_hbm.at[0, c], kbuf.at[c], k_sem.at[1])
    fetch("v1", v_hbm.at[0, c], vbuf.at[c], v_sem.at[1])
    fetch("fk", fk_hbm.at[0, c], fkbuf, f_sem.at[0])
    fetch("fv", fv_hbm.at[0, c], fvbuf, f_sem.at[1])

    pl.semaphore_wait(barrier, len(peers))

    q_copies = []
    for at, head in enumerate((c, other)):
        q_copies.append(
            pltpu.make_async_remote_copy(
                src_ref=q_hbm.at[0, head],
                dst_ref=qbuf.at[head, mine, :],
                send_sem=qx_send.at[at],
                recv_sem=qx_recv.at[at],
                device_id=partner,
                device_id_type=MESH,
            )
        )
        q_copies[-1].start()

    depth = w_hbm.shape[0] // 2
    piece = depth // WCUT
    for at, head in enumerate((c, other)):
        for cut in range(WCUT):
            fetch(
                ("w", at, cut),
                w_hbm.at[pl.ds(pl.multiple_of(head * depth + cut * piece, piece), piece), :],
                wbuf.at[head, pl.ds(cut * piece, piece), :],
                w_sem.at[at, cut],
            )

    local["pos"].wait()
    length = len_ref[0]
    first_slot = c * slots

    def scores(query, head):
        fold = jnp.full((query.shape[0], 128), NEG, f32)
        for at in range(slots // CHUNK):
            span = slice(at * CHUNK, (at + 1) * CHUNK)
            part = lax.dot_general(
                query, kbuf[head, span, :], (((1,), (1,)), ((), ())), preferred_element_type=f32
            )
            slot = first_slot + at * CHUNK + lax.broadcasted_iota(jnp.int32, (1, CHUNK), 1)
            part = part + jnp.where(slot < length, 0.0, NEG)
            sbuf[0 : query.shape[0], span] = part
            for lane in range(CHUNK // 128):
                fold = jnp.maximum(fold, part[:, lane * 128 : (lane + 1) * 128])
        return jnp.max(fold, axis=1, keepdims=True)

    def weighted(count, head, top):
        ones = jnp.ones((CHUNK, 128), bf16)
        acc = jnp.zeros((count, head_size + 128), f32)
        for at in range(slots // CHUNK):
            span = slice(at * CHUNK, (at + 1) * CHUNK)
            weights = jnp.exp2((sbuf[0:count, span] - top) * factor).astype(bf16)
            both = jnp.concatenate([vbuf[head, span, :], ones], axis=1)
            acc = acc + jnp.dot(weights, both, preferred_element_type=f32)
        return acc[:, :head_size], acc[:, head_size:]

    lane = lax.broadcasted_iota(jnp.int32, (half, 128), 1)
    p_copies, s_copies = [], []

    def give_back(at, side):
        query = qbuf[other, pl.ds(pl.multiple_of(side * half, half), half), :]
        top = scores(query, other)
        if at == 0:
            local["v0"].wait()
        summed, total = weighted(half, other, top)
        po_send[side] = summed.astype(bf16)
        turned = jnp.transpose(jnp.where(lane < 64, jnp.broadcast_to(top, (half, 128)), total))
        st_send[side, 0:8, :] = turned[0:8, :]
        st_send[side, 8:16, :] = turned[64:72, :]
        p_copies.append(
            pltpu.make_async_remote_copy(
                src_ref=po_send.at[side], dst_ref=po_recv.at[side],
                send_sem=px_send.at[at], recv_sem=px_recv.at[at],
                device_id=partner, device_id_type=MESH,
            )
        )
        s_copies.append(
            pltpu.make_async_remote_copy(
                src_ref=st_send.at[side], dst_ref=st_recv.at[side],
                send_sem=sx_send.at[at], recv_sem=sx_recv.at[at],
                device_id=partner, device_id_type=MESH,
            )
        )
        s_copies[-1].start()
        p_copies[-1].start()

    token_here = lax.broadcasted_iota(jnp.int32, (half, NEW), 0) // QPK
    fresh_at = lax.broadcasted_iota(jnp.int32, (half, NEW), 1)

    def keep(at, side):
        token = token_here + side * (half // QPK)
        row_pos = jnp.zeros((half, NEW), jnp.int32)
        new_pos = jnp.zeros((half, NEW), jnp.int32)
        for t in range(NEW):
            value = pos_ref[0, t]
            row_pos = jnp.where(token == t, value, row_pos)
            new_pos = jnp.where(fresh_at == t, value, new_pos)
        allow = new_pos <= row_pos
        query = qbuf[c, pl.ds(pl.multiple_of(side * half, half), half), :]
        top = scores(query, c)
        fresh = lax.dot_general(
            query, fkbuf[...], (((1,), (1,)), ((), ())), preferred_element_type=f32
        )
        fresh = jnp.where(allow, fresh, NEG)
        top = jnp.maximum(top, jnp.max(fresh, axis=1, keepdims=True))
        if at == 0:
            local["v1"].wait()
            local["fv"].wait()
        summed, total = weighted(half, c, top)
        fresh_weights = jnp.where(allow, jnp.exp2((fresh - top) * factor), 0.0).astype(bf16)
        summed = summed + jnp.dot(fresh_weights, fvbuf[...], preferred_element_type=f32)
        total = total + jnp.sum(fresh_weights.astype(f32), axis=1, keepdims=True)
        return jnp.broadcast_to(top, (half, 128)), total, summed

    def merge(side, state):
        top_here, total, summed = state
        top_there = jnp.transpose(jnp.broadcast_to(st_recv[side, 0:1, :], (128, half)))
        total_there = jnp.transpose(jnp.broadcast_to(st_recv[side, 8:9, :], (128, half)))
        best = jnp.maximum(top_here, top_there)
        here = jnp.exp2((top_here - best) * factor)
        there = jnp.exp2((top_there - best) * factor)
        num = summed * here + po_recv[side].astype(f32) * there
        den = total * here + total_there * there
        fbuf[pl.ds(pl.multiple_of(side * half, half), half), :] = num / den

    local["q"].wait()
    local["k0"].wait()
    give_back(0, c)
    local["k1"].wait()
    local["fk"].wait()
    state_mine = keep(0, c)
    q_copies[0].wait_recv()
    give_back(1, other)
    q_copies[1].wait_recv()
    state_other = keep(1, other)

    s_copies[0].wait_recv()
    p_copies[0].wait_recv()
    merge(other, state_other)
    s_copies[1].wait_recv()
    p_copies[1].wait_recv()
    merge(c, state_mine)
    for j in range(QPK):
        feature = fbuf[pl.ds(j, NEW, stride=QPK), :]
        gather[c, r, :, j * head_size : (j + 1) * head_size] = feature.astype(bf16)

    def pass_on(at, slot_c, slot_r, peer):
        block = gather.at[slot_c, slot_r]
        copy = pltpu.make_async_remote_copy(
            src_ref=block, dst_ref=block,
            send_sem=g_send.at[at], recv_sem=g_recv.at[at],
            device_id=peer, device_id_type=MESH,
        )
        copy.start()
        return copy

    g_far = pass_on(0, c, r, {"roll": far})
    g_sib = pass_on(1, c, r, {"roll": sib})
    g_ctx = pass_on(2, c, r, partner)
    g_diag = pass_on(3, c, r, {"ctx": other, "roll": far})
    g_far.wait_recv()
    f_far = pass_on(4, c, far, {"roll": sib})
    g_ctx.wait_recv()
    f_ctx = pass_on(5, other, r, {"roll": sib})
    for at in range(2):
        for cut in range(WCUT):
            local[("w", at, cut)].wait()
    g_sib.wait_recv()
    f_far.wait_recv()

    n_cols = wbuf.shape[2] // COLS
    tokens = gather.shape[1] * NEW

    def project(head, at):
        features = gather[head].reshape(tokens, depth)
        return jnp.dot(
            features, wbuf[head, :, at * COLS : (at + 1) * COLS], preferred_element_type=f32
        )

    f_diag = None
    for at in range(n_cols):
        accbuf[:, at * COLS : (at + 1) * COLS] = project(c, at)
        if at == n_cols // 2 - 1:
            g_diag.wait_recv()
            f_diag = pass_on(6, other, far, {"roll": sib})
    f_ctx.wait_recv()
    f_diag.wait_recv()

    odd = lax.rem(h, 2)
    across, near = n_head - 1 - h, h + 1 - 2 * odd
    middle = jnp.logical_and(h > 0, h < n_head - 1)
    rs_copies = []

    def hand_over(at, block, to, slot):
        span = slice(at * COLS, (at + 1) * COLS)
        return pltpu.make_async_remote_copy(
            src_ref=rs_send.at[block, :, span],
            dst_ref=rs_recv.at[slot, :, span],
            send_sem=rs_send_sem.at[slot, at],
            recv_sem=rs_recv_sem.at[slot, at],
            device_id={"head": to},
            device_id_type=MESH,
        )

    def arrived(at, slot):
        hand_over(at, across, across, slot).wait_recv()

    def add_and_cross(at):
        span = slice(at * COLS, (at + 1) * COLS)
        arrived(at, 1)
        theirs = pl.ds(pl.multiple_of(across * NEW, NEW), NEW)
        part = accbuf[theirs, span] + rs_recv[1, :, span].astype(f32)
        rs_send[across, :, span] = part.astype(bf16)
        rs_copies[at][1].start()

    for at in range(n_cols):
        span = slice(at * COLS, (at + 1) * COLS)
        part = accbuf[:, span] + project(other, at)
        accbuf[:, span] = part
        rs_send[:, :, span] = part.astype(bf16).reshape(n_head, NEW, COLS)
        two = hand_over(at, lax.rem(h + 2, n_head), lax.rem(2 * h + 1, n_head + 1), 1)
        cross = hand_over(at, across, across, 2 - 2 * odd)
        side = hand_over(at, near, near, 2 * odd)
        rs_copies.append((two, cross, side))
        two.start()
        pl.when(jnp.logical_not(middle))(cross.start)
        side.start()
        if at > 0:
            pl.when(middle)(functools.partial(add_and_cross, at - 1))
    pl.when(middle)(functools.partial(add_and_cross, n_cols - 1))

    own = pl.ds(pl.multiple_of(h * NEW, NEW), NEW)

    def add_third(at):
        span = slice(at * COLS, (at + 1) * COLS)
        arrived(at, 1)
        accbuf[own, span] += rs_recv[1, :, span].astype(f32)

    for at in range(n_cols):
        span = slice(at * COLS, (at + 1) * COLS)
        pl.when(jnp.logical_not(middle))(functools.partial(add_third, at))
        arrived(at, 0)
        arrived(at, 2)
        value = accbuf[own, span] + rs_recv[0, :, span].astype(f32) + rs_recv[2, :, span].astype(f32)
        out_ref[0, :, span] = value.astype(bf16)

    for copy in q_copies + p_copies + s_copies:
        copy.wait_send()
    for copy in (g_far, g_sib, g_ctx, g_diag, f_far, f_ctx, f_diag):
        copy.wait_send()
    for copies in rs_copies:
        for copy in copies:
            copy.wait_send()


def fused_body(n_head, queries, cache_keys, cache_values, new_keys, new_values, lengths, positions, out_weight):
    f32, bf16 = jnp.float32, jnp.bfloat16
    _, heads, slots, head_size = cache_keys.shape
    half = queries.shape[2]
    rows = 2 * half
    width = out_weight.shape[1]
    depth = out_weight.shape[0] // heads
    n_cols = width // COLS
    dma = pltpu.SemaphoreType.DMA
    pinned = [
        pltpu.with_memory_space_constraint(array, pltpu.HBM)
        for array in (queries, cache_keys, cache_values, new_keys, new_values, positions)
    ]
    anywhere = pl.BlockSpec(memory_space=pltpu.HBM)
    return pl.pallas_call(
        functools.partial(fused_kernel, n_head),
        out_shape=jax.ShapeDtypeStruct((1, NEW, width), bf16),
        in_specs=[anywhere] * 5 + [pl.BlockSpec(memory_space=pltpu.SMEM)] + [anywhere] * 2,
        out_specs=pl.BlockSpec(memory_space=pltpu.VMEM),
        scratch_shapes=[
            pltpu.SMEM(positions.shape, positions.dtype),
            pltpu.VMEM((heads, rows, head_size), bf16),
            pltpu.VMEM((heads, slots, head_size), bf16),
            pltpu.VMEM((heads, slots, head_size), bf16),
            pltpu.VMEM((NEW, head_size), bf16),
            pltpu.VMEM((NEW, head_size), bf16),
            pltpu.VMEM((heads, depth, width), bf16),
            pltpu.VMEM((half, slots), f32),
            pltpu.VMEM((2, half, head_size), bf16),
            pltpu.VMEM((2, half, head_size), bf16),
            pltpu.VMEM((2, 16, half), f32),
            pltpu.VMEM((2, 16, half), f32),
            pltpu.VMEM((rows, head_size), f32),
            pltpu.VMEM((2, 4, NEW, depth), bf16),
            pltpu.VMEM((4 * NEW, width), f32),
            pltpu.VMEM((n_head, NEW, width), bf16),
            pltpu.VMEM((n_head - 1, NEW, width), bf16),
            dma, dma((2,)), dma((2,)), dma((2,)), dma, dma((2, WCUT)),
            dma((2,)), dma((2,)), dma((2,)), dma((2,)), dma((2,)), dma((2,)),
            dma((7,)), dma((7,)),
            dma((n_head - 1, n_cols)), dma((n_head - 1, n_cols)),
        ],
        compiler_params=pltpu.CompilerParams(
            collective_id=0, has_side_effects=True, vmem_limit_bytes=48 * 1024 * 1024
        ),
        cost_estimate=pl.CostEstimate(
            flops=4 * heads * rows * slots * head_size + 2 * 4 * NEW * heads * depth * width,
            bytes_accessed=2 * heads * (2 * slots * head_size + depth * width),
            transcendentals=heads * rows * slots,
        ),
    )(*pinned[:5], lengths, pinned[5], out_weight)


def shifted(value, axis, steps):
    count = lax.axis_size(axis)
    pairs = [(source, (source + steps) % count) for source in range(count)]
    return lax.ppermute(value, axis, pairs)


def ring_body(queries, cache_keys, cache_values, new_keys, new_values, lengths, positions, out_weight):
    here = lax.axis_index("ctx")
    n_ctx = lax.axis_size("ctx")
    slots = cache_keys.shape[2]
    head_size = cache_keys.shape[3]
    local_heads = cache_keys.shape[1]
    scale = 1.0 / head_size**0.5
    keys = cache_keys[0]
    values = cache_values[0]
    fresh_keys = new_keys[0]
    fresh_values = new_values[0]
    pos = positions[0]
    slot_ok = here * slots + jnp.arange(slots) < lengths[0]

    def update(state, block, first_row, use_new):
        top_old, total_old, summed_old = state
        count = block.shape[1]
        scores = jnp.einsum("krd,ksd->krs", block, keys, preferred_element_type=jnp.float32) * scale
        scores = jnp.where(slot_ok[None, None, :], scores, NEG)
        fresh = (
            jnp.einsum("krd,kud->kru", block, fresh_keys, preferred_element_type=jnp.float32)
            * scale
        )
        token = (first_row + jnp.arange(count)) // QPK
        allow = jnp.logical_and(pos[None, :] <= pos[token][:, None], use_new)
        fresh = jnp.where(allow[None], fresh, NEG)
        top = jnp.maximum(top_old, jnp.maximum(jnp.max(scores, axis=2), jnp.max(fresh, axis=2)))
        cache_weights = jnp.where(
            slot_ok[None, None, :], jnp.exp(scores - top[..., None]), 0.0
        ).astype(jnp.bfloat16)
        fresh_weights = jnp.where(allow[None], jnp.exp(fresh - top[..., None]), 0.0).astype(
            jnp.bfloat16
        )
        factor = jnp.exp(top_old - top)
        total = total_old * factor + jnp.sum(cache_weights.astype(jnp.float32), axis=2)
        total = total + jnp.sum(fresh_weights.astype(jnp.float32), axis=2)
        summed = summed_old * factor[..., None]
        summed = summed + jnp.einsum(
            "krs,ksd->krd", cache_weights, values, preferred_element_type=jnp.float32
        )
        summed = summed + jnp.einsum(
            "kru,kud->krd", fresh_weights, fresh_values, preferred_element_type=jnp.float32
        )
        return (top, total, summed)

    block = queries[0]
    block_rows = block.shape[1]
    state = update(
        (
            jnp.full((local_heads, block_rows), NEG, jnp.float32),
            jnp.zeros((local_heads, block_rows), jnp.float32),
            jnp.zeros((local_heads, block_rows, head_size), jnp.float32),
        ),
        block,
        here * block_rows,
        True,
    )

    def turn(step, carry):
        moving, top, total, summed = carry
        moving = shifted(moving, "ctx", 1)
        top, total, summed = shifted((top, total, summed), "ctx", 1)
        top, total, summed = update((top, total, summed), moving, 0, False)
        return (moving, top, total, summed)

    moving, top, total, summed = lax.fori_loop(
        0, n_ctx - 1, turn, (block, state[0], state[1], state[2])
    )
    attended = (summed / total[..., None]).astype(jnp.bfloat16)
    every = lax.all_gather(attended[None], ("ctx", "roll"), axis=0, tiled=True)
    n_roll = every.shape[0] // n_ctx
    every = every.reshape(n_ctx, n_roll, local_heads, block_rows, head_size)
    every = jnp.roll(every, 1, axis=0)
    rows_all = every.transpose(1, 2, 0, 3, 4).reshape(
        n_roll, local_heads, n_ctx * block_rows, head_size
    )
    n_roll = rows_all.shape[0]
    features = rows_all.reshape(n_roll, local_heads, NEW, QPK, head_size).transpose(0, 2, 1, 3, 4)
    features = features.reshape(n_roll, NEW, local_heads * QPK * head_size)
    return lax.psum_scatter(
        jnp.einsum("rtf,fc->rtc", features, out_weight, preferred_element_type=jnp.float32).astype(
            jnp.bfloat16
        ),
        "head",
        scatter_dimension=0,
        tiled=True,
    )


def solution(mesh):
    in_specs = (
        P("roll", "head", "ctx", None),
        P("roll", "head", "ctx", None),
        P("roll", "head", "ctx", None),
        P("roll", "head", None, None),
        P("roll", "head", None, None),
        P("roll"),
        P("roll", None),
        P("head", ("ctx", "roll")),
    )
    out_specs = P("head", None, ("ctx", "roll"))
    body = ring_body
    if (mesh.shape["ctx"], mesh.shape["head"], mesh.shape["roll"]) == (2, 4, 4):
        body = functools.partial(fused_body, mesh.shape["head"])
    return jax.shard_map(body, mesh=mesh, in_specs=in_specs, out_specs=out_specs, check_vma=False)
```

```python
import functools
import math

import jax
import jax.numpy as jnp
from jax import lax
from jax.experimental import pallas as pl
from jax.experimental.pallas import tpu as pltpu
from jax.sharding import PartitionSpec as P

NEW = 16
QPK = 16


NEG = -1e30

MESH = pl.DeviceIdType.MESH
CHUNK = 512
COLS = 512


def fused_kernel(
    n_head,
    q_hbm, k_hbm, v_hbm, fk_hbm, fv_hbm, len_ref, pos_hbm, w_hbm,
    out_ref,
    pos_ref, qbuf, kbuf, vbuf, fkbuf, fvbuf, wbuf, sbuf,
    po_send, po_recv, st_send, st_recv, fbuf, gather, accbuf, rs_send, rs_recv,
    q_sem, k_sem, v_sem, f_sem, n_sem, w_sem,
    qx_send, qx_recv, px_send, px_recv, sx_send, sx_recv,
    g_send, g_recv, rs_send_sem, rs_recv_sem,
):
    f32, bf16 = jnp.float32, jnp.bfloat16
    c, h, r = lax.axis_index("ctx"), lax.axis_index("head"), lax.axis_index("roll")
    other = 1 - c
    sib = r + 1 - 2 * lax.rem(r, 2)
    far = lax.rem(r + 2, 4)
    far_sib = lax.rem(sib + 2, 4)
    partner = {"ctx": other}
    rows, head_size = qbuf.shape[1], qbuf.shape[2]
    half = rows // 2
    slots = kbuf.shape[1]
    factor = math.log2(math.e) / math.sqrt(head_size)

    barrier = pltpu.get_barrier_semaphore()
    peers = [partner, {"roll": sib}, {"roll": far}, {"ctx": other, "roll": far}]
    peers += [{"head": lax.rem(h + off, n_head)} for off in range(1, n_head)]
    for peer in peers:
        pl.semaphore_signal(barrier, inc=1, device_id=peer, device_id_type=MESH)

    local = {}

    def fetch(name, src, dst, sem):
        local[name] = pltpu.make_async_copy(src, dst, sem)
        local[name].start()

    mine = pl.ds(pl.multiple_of(c * half, half), half)
    fetch("q", q_hbm.at[0], qbuf.at[:, mine, :], q_sem)
    fetch("k0", k_hbm.at[0, other], kbuf.at[other], k_sem.at[0])
    fetch("v0", v_hbm.at[0, other], vbuf.at[other], v_sem.at[0])
    fetch("pos", pos_hbm, pos_ref, n_sem)
    fetch("k1", k_hbm.at[0, c], kbuf.at[c], k_sem.at[1])
    fetch("v1", v_hbm.at[0, c], vbuf.at[c], v_sem.at[1])
    fetch("fk", fk_hbm.at[0, c], fkbuf, f_sem.at[0])
    fetch("fv", fv_hbm.at[0, c], fvbuf, f_sem.at[1])

    pl.semaphore_wait(barrier, len(peers))

    q_copies = []
    for at, head in enumerate((c, other)):
        q_copies.append(
            pltpu.make_async_remote_copy(
                src_ref=q_hbm.at[0, head],
                dst_ref=qbuf.at[head, mine, :],
                send_sem=qx_send.at[at],
                recv_sem=qx_recv.at[at],
                device_id=partner,
                device_id_type=MESH,
            )
        )
        q_copies[-1].start()

    depth = w_hbm.shape[0] // 2
    for at, head in enumerate((c, other)):
        for cut in range(wbuf.shape[2] // COLS):
            span = pl.ds(cut * COLS, COLS)
            fetch(
                ("w", at, cut),
                w_hbm.at[pl.ds(pl.multiple_of(head * depth, depth), depth), span],
                wbuf.at[head, :, span],
                w_sem.at[at, cut],
            )

    local["pos"].wait()
    length = len_ref[0]
    first_slot = c * slots

    def scores(query, head):
        fold = jnp.full((query.shape[0], 128), NEG, f32)
        for at in range(slots // CHUNK):
            span = slice(at * CHUNK, (at + 1) * CHUNK)
            part = lax.dot_general(
                query, kbuf[head, span, :], (((1,), (1,)), ((), ())), preferred_element_type=f32
            )
            slot = first_slot + at * CHUNK + lax.broadcasted_iota(jnp.int32, (1, CHUNK), 1)
            part = part + jnp.where(slot < length, 0.0, NEG)
            sbuf[0 : query.shape[0], span] = part
            for lane in range(CHUNK // 128):
                fold = jnp.maximum(fold, part[:, lane * 128 : (lane + 1) * 128])
        return jnp.max(fold, axis=1, keepdims=True)

    def weighted(count, head, top):
        ones = jnp.ones((CHUNK, 128), bf16)
        acc = jnp.zeros((count, head_size + 128), f32)
        for at in range(slots // CHUNK):
            span = slice(at * CHUNK, (at + 1) * CHUNK)
            weights = jnp.exp2((sbuf[0:count, span] - top) * factor).astype(bf16)
            both = jnp.concatenate([vbuf[head, span, :], ones], axis=1)
            acc = acc + jnp.dot(weights, both, preferred_element_type=f32)
        return acc[:, :head_size], acc[:, head_size:]

    lane = lax.broadcasted_iota(jnp.int32, (half, 128), 1)
    p_copies, s_copies = [], []

    def give_back(at, side):
        query = qbuf[other, pl.ds(pl.multiple_of(side * half, half), half), :]
        top = scores(query, other)
        if at == 0:
            local["v0"].wait()
        summed, total = weighted(half, other, top)
        po_send[side] = summed.astype(bf16)
        p_copies.append(
            pltpu.make_async_remote_copy(
                src_ref=po_send.at[side], dst_ref=po_recv.at[side],
                send_sem=px_send.at[at], recv_sem=px_recv.at[at],
                device_id=partner, device_id_type=MESH,
            )
        )
        p_copies[-1].start()
        turned = jnp.transpose(jnp.where(lane < 64, jnp.broadcast_to(top, (half, 128)), total))
        st_send[side, 0:8, :] = turned[0:8, :]
        st_send[side, 8:16, :] = turned[64:72, :]
        s_copies.append(
            pltpu.make_async_remote_copy(
                src_ref=st_send.at[side], dst_ref=st_recv.at[side],
                send_sem=sx_send.at[at], recv_sem=sx_recv.at[at],
                device_id=partner, device_id_type=MESH,
            )
        )
        s_copies[-1].start()

    token_here = lax.broadcasted_iota(jnp.int32, (half, NEW), 0) // QPK
    fresh_at = lax.broadcasted_iota(jnp.int32, (half, NEW), 1)

    def new_mask(side):
        token = token_here + side * (half // QPK)
        row_pos = jnp.zeros((half, NEW), jnp.int32)
        new_pos = jnp.zeros((half, NEW), jnp.int32)
        for t in range(NEW):
            value = pos_ref[0, t]
            row_pos = jnp.where(token == t, value, row_pos)
            new_pos = jnp.where(fresh_at == t, value, new_pos)
        return new_pos <= row_pos

    def keep(at, side, allow):
        query = qbuf[c, pl.ds(pl.multiple_of(side * half, half), half), :]
        top = scores(query, c)
        fresh = lax.dot_general(
            query, fkbuf[...], (((1,), (1,)), ((), ())), preferred_element_type=f32
        )
        fresh = jnp.where(allow, fresh, NEG)
        top = jnp.maximum(top, jnp.max(fresh, axis=1, keepdims=True))
        if at == 0:
            local["v1"].wait()
            local["fv"].wait()
        summed, total = weighted(half, c, top)
        fresh_weights = jnp.where(allow, jnp.exp2((fresh - top) * factor), 0.0).astype(bf16)
        summed = summed + jnp.dot(fresh_weights, fvbuf[...], preferred_element_type=f32)
        total = total + jnp.sum(fresh_weights.astype(f32), axis=1, keepdims=True)
        return jnp.broadcast_to(top, (half, 128)), total, summed

    def merge(side, state):
        top_here, total, summed = state
        top_there = jnp.transpose(jnp.broadcast_to(st_recv[side, 0:1, :], (128, half)))
        total_there = jnp.transpose(jnp.broadcast_to(st_recv[side, 8:9, :], (128, half)))
        best = jnp.maximum(top_here, top_there)
        here = jnp.exp2((top_here - best) * factor)
        there = jnp.exp2((top_there - best) * factor)
        num = summed * here + po_recv[side].astype(f32) * there
        den = total * here + total_there * there
        fbuf[pl.ds(pl.multiple_of(side * half, half), half), :] = num / den

    local["q"].wait()
    local["k0"].wait()
    give_back(0, c)
    local["k1"].wait()
    local["fk"].wait()
    state_mine = keep(0, c, new_mask(c))
    mask_other = new_mask(other)
    q_copies[0].wait_recv()
    give_back(1, other)
    q_copies[1].wait_recv()
    state_other = keep(1, other, mask_other)

    s_copies[0].wait_recv()
    p_copies[0].wait_recv()
    merge(other, state_other)
    s_copies[1].wait_recv()
    p_copies[1].wait_recv()
    merge(c, state_mine)
    for j in range(QPK):
        feature = fbuf[pl.ds(j, NEW, stride=QPK), :]
        gather[c, r, :, j * head_size : (j + 1) * head_size] = feature.astype(bf16)

    def pass_on(at, slot_c, slot_r, peer):
        block = gather.at[slot_c, slot_r]
        copy = pltpu.make_async_remote_copy(
            src_ref=block, dst_ref=block,
            send_sem=g_send.at[at], recv_sem=g_recv.at[at],
            device_id=peer, device_id_type=MESH,
        )
        copy.start()
        return copy

    g_far = pass_on(0, c, r, {"roll": far})
    g_sib = pass_on(1, c, r, {"roll": sib})
    g_ctx = pass_on(2, c, r, partner)
    g_diag = pass_on(3, c, r, {"ctx": other, "roll": far})
    g_far.wait_recv()
    f_far = pass_on(4, c, far, {"roll": sib})
    g_ctx.wait_recv()
    f_ctx = pass_on(5, other, r, {"roll": sib})
    g_sib.wait_recv()
    f_far.wait_recv()

    n_cols = wbuf.shape[2] // COLS
    tokens = gather.shape[1] * NEW

    def project(head, at):
        features = gather[head].reshape(tokens, depth)
        return jnp.dot(
            features, wbuf[head, :, at * COLS : (at + 1) * COLS], preferred_element_type=f32
        )

    f_diag = None
    for at in range(n_cols):
        local[("w", 0, at)].wait()
        accbuf[:, at * COLS : (at + 1) * COLS] = project(c, at)
        if at == n_cols // 2 - 1:
            g_diag.wait_recv()
            f_diag = pass_on(6, other, far, {"roll": sib})
    f_ctx.wait_recv()
    f_diag.wait_recv()

    rs_copies = []
    for at in range(n_cols):
        span = slice(at * COLS, (at + 1) * COLS)
        local[("w", 1, at)].wait()
        part = accbuf[:, span] + project(other, at)
        accbuf[:, span] = part
        rs_send[:, :, span] = part.astype(bf16).reshape(n_head, NEW, COLS)
        for off in range(n_head - 1, 0, -1):
            to = lax.rem(h + off, n_head)
            copy = pltpu.make_async_remote_copy(
                src_ref=rs_send.at[to, :, span],
                dst_ref=rs_recv.at[off - 1, :, span],
                send_sem=rs_send_sem.at[off - 1, at],
                recv_sem=rs_recv_sem.at[off - 1, at],
                device_id={"head": to},
                device_id_type=MESH,
            )
            copy.start()
            rs_copies.append((at, copy))

    own = pl.ds(pl.multiple_of(h * NEW, NEW), NEW)
    for at in range(n_cols):
        span = slice(at * COLS, (at + 1) * COLS)
        for place, copy in rs_copies:
            if place == at:
                copy.wait_recv()
        value = accbuf[own, span]
        for off in range(n_head - 1):
            value = value + rs_recv[off, :, span].astype(f32)
        out_ref[0, :, span] = value.astype(bf16)

    for copy in q_copies + p_copies + s_copies:
        copy.wait_send()
    for copy in (g_far, g_sib, g_ctx, g_diag, f_far, f_ctx, f_diag):
        copy.wait_send()
    for _, copy in rs_copies:
        copy.wait_send()


def fused_body(n_head, queries, cache_keys, cache_values, new_keys, new_values, lengths, positions, out_weight):
    f32, bf16 = jnp.float32, jnp.bfloat16
    _, heads, slots, head_size = cache_keys.shape
    half = queries.shape[2]
    rows = 2 * half
    width = out_weight.shape[1]
    depth = out_weight.shape[0] // heads
    n_cols = width // COLS
    dma = pltpu.SemaphoreType.DMA
    pinned = [
        pltpu.with_memory_space_constraint(array, pltpu.HBM)
        for array in (queries, cache_keys, cache_values, new_keys, new_values, positions)
    ]
    anywhere = pl.BlockSpec(memory_space=pltpu.HBM)
    return pl.pallas_call(
        functools.partial(fused_kernel, n_head),
        out_shape=jax.ShapeDtypeStruct((1, NEW, width), bf16),
        in_specs=[anywhere] * 5 + [pl.BlockSpec(memory_space=pltpu.SMEM)] + [anywhere] * 2,
        out_specs=pl.BlockSpec(memory_space=pltpu.VMEM),
        scratch_shapes=[
            pltpu.SMEM(positions.shape, positions.dtype),
            pltpu.VMEM((heads, rows, head_size), bf16),
            pltpu.VMEM((heads, slots, head_size), bf16),
            pltpu.VMEM((heads, slots, head_size), bf16),
            pltpu.VMEM((NEW, head_size), bf16),
            pltpu.VMEM((NEW, head_size), bf16),
            pltpu.VMEM((heads, depth, width), bf16),
            pltpu.VMEM((half, slots), f32),
            pltpu.VMEM((2, half, head_size), bf16),
            pltpu.VMEM((2, half, head_size), bf16),
            pltpu.VMEM((2, 16, half), f32),
            pltpu.VMEM((2, 16, half), f32),
            pltpu.VMEM((rows, head_size), f32),
            pltpu.VMEM((2, 4, NEW, depth), bf16),
            pltpu.VMEM((4 * NEW, width), f32),
            pltpu.VMEM((n_head, NEW, width), bf16),
            pltpu.VMEM((n_head - 1, NEW, width), bf16),
            dma, dma((2,)), dma((2,)), dma((2,)), dma, dma((2, n_cols)),
            dma((2,)), dma((2,)), dma((2,)), dma((2,)), dma((2,)), dma((2,)),
            dma((7,)), dma((7,)),
            dma((n_head - 1, n_cols)), dma((n_head - 1, n_cols)),
        ],
        compiler_params=pltpu.CompilerParams(
            collective_id=0, has_side_effects=True, vmem_limit_bytes=48 * 1024 * 1024
        ),
        cost_estimate=pl.CostEstimate(
            flops=4 * heads * rows * slots * head_size + 2 * 4 * NEW * heads * depth * width,
            bytes_accessed=2 * heads * (2 * slots * head_size + depth * width),
            transcendentals=heads * rows * slots,
        ),
    )(*pinned[:5], lengths, pinned[5], out_weight)


def shifted(value, axis, steps):
    count = lax.axis_size(axis)
    pairs = [(source, (source + steps) % count) for source in range(count)]
    return lax.ppermute(value, axis, pairs)


def ring_body(queries, cache_keys, cache_values, new_keys, new_values, lengths, positions, out_weight):
    here = lax.axis_index("ctx")
    n_ctx = lax.axis_size("ctx")
    slots = cache_keys.shape[2]
    head_size = cache_keys.shape[3]
    local_heads = cache_keys.shape[1]
    scale = 1.0 / head_size**0.5
    keys = cache_keys[0]
    values = cache_values[0]
    fresh_keys = new_keys[0]
    fresh_values = new_values[0]
    pos = positions[0]
    slot_ok = here * slots + jnp.arange(slots) < lengths[0]

    def update(state, block, first_row, use_new):
        top_old, total_old, summed_old = state
        count = block.shape[1]
        scores = jnp.einsum("krd,ksd->krs", block, keys, preferred_element_type=jnp.float32) * scale
        scores = jnp.where(slot_ok[None, None, :], scores, NEG)
        fresh = (
            jnp.einsum("krd,kud->kru", block, fresh_keys, preferred_element_type=jnp.float32)
            * scale
        )
        token = (first_row + jnp.arange(count)) // QPK
        allow = jnp.logical_and(pos[None, :] <= pos[token][:, None], use_new)
        fresh = jnp.where(allow[None], fresh, NEG)
        top = jnp.maximum(top_old, jnp.maximum(jnp.max(scores, axis=2), jnp.max(fresh, axis=2)))
        cache_weights = jnp.where(
            slot_ok[None, None, :], jnp.exp(scores - top[..., None]), 0.0
        ).astype(jnp.bfloat16)
        fresh_weights = jnp.where(allow[None], jnp.exp(fresh - top[..., None]), 0.0).astype(
            jnp.bfloat16
        )
        factor = jnp.exp(top_old - top)
        total = total_old * factor + jnp.sum(cache_weights.astype(jnp.float32), axis=2)
        total = total + jnp.sum(fresh_weights.astype(jnp.float32), axis=2)
        summed = summed_old * factor[..., None]
        summed = summed + jnp.einsum(
            "krs,ksd->krd", cache_weights, values, preferred_element_type=jnp.float32
        )
        summed = summed + jnp.einsum(
            "kru,kud->krd", fresh_weights, fresh_values, preferred_element_type=jnp.float32
        )
        return (top, total, summed)

    block = queries[0]
    block_rows = block.shape[1]
    state = update(
        (
            jnp.full((local_heads, block_rows), NEG, jnp.float32),
            jnp.zeros((local_heads, block_rows), jnp.float32),
            jnp.zeros((local_heads, block_rows, head_size), jnp.float32),
        ),
        block,
        here * block_rows,
        True,
    )

    def turn(step, carry):
        moving, top, total, summed = carry
        moving = shifted(moving, "ctx", 1)
        top, total, summed = shifted((top, total, summed), "ctx", 1)
        top, total, summed = update((top, total, summed), moving, 0, False)
        return (moving, top, total, summed)

    moving, top, total, summed = lax.fori_loop(
        0, n_ctx - 1, turn, (block, state[0], state[1], state[2])
    )
    attended = (summed / total[..., None]).astype(jnp.bfloat16)
    every = lax.all_gather(attended[None], ("ctx", "roll"), axis=0, tiled=True)
    n_roll = every.shape[0] // n_ctx
    every = every.reshape(n_ctx, n_roll, local_heads, block_rows, head_size)
    every = jnp.roll(every, 1, axis=0)
    rows_all = every.transpose(1, 2, 0, 3, 4).reshape(
        n_roll, local_heads, n_ctx * block_rows, head_size
    )
    n_roll = rows_all.shape[0]
    features = rows_all.reshape(n_roll, local_heads, NEW, QPK, head_size).transpose(0, 2, 1, 3, 4)
    features = features.reshape(n_roll, NEW, local_heads * QPK * head_size)
    return lax.psum_scatter(
        jnp.einsum("rtf,fc->rtc", features, out_weight, preferred_element_type=jnp.float32).astype(
            jnp.bfloat16
        ),
        "head",
        scatter_dimension=0,
        tiled=True,
    )


def solution(mesh):
    in_specs = (
        P("roll", "head", "ctx", None),
        P("roll", "head", "ctx", None),
        P("roll", "head", "ctx", None),
        P("roll", "head", None, None),
        P("roll", "head", None, None),
        P("roll"),
        P("roll", None),
        P("head", ("ctx", "roll")),
    )
    out_specs = P("head", None, ("ctx", "roll"))
    body = ring_body
    if (mesh.shape["ctx"], mesh.shape["head"], mesh.shape["roll"]) == (2, 4, 4):
        body = functools.partial(fused_body, mesh.shape["head"])
    return jax.shard_map(body, mesh=mesh, in_specs=in_specs, out_specs=out_specs, check_vma=False)
```

```python
import functools
import math

import jax
import jax.numpy as jnp
from jax import lax
from jax.experimental import pallas as pl
from jax.experimental.pallas import tpu as pltpu
from jax.sharding import PartitionSpec as P

NEW = 16
QPK = 16


NEG = -1e30

MESH = pl.DeviceIdType.MESH
CHUNK = 512
COLS = 256
WIDE = 512


def fused_kernel(
    n_head,
    q_hbm, k_hbm, v_hbm, fk_hbm, fv_hbm, len_ref, pos_hbm, w_hbm,
    out_ref,
    pos_ref, qbuf, kbuf, vbuf, fkbuf, fvbuf, wbuf, sbuf,
    po_send, po_recv, st_send, st_recv, fbuf, gather, accbuf, rs_send, rs_recv,
    q_sem, k_sem, v_sem, f_sem, n_sem, w_sem,
    qx_send, qx_recv, px_send, px_recv, sx_send, sx_recv,
    g_send, g_recv, rs_send_sem, rs_recv_sem,
):
    f32, bf16 = jnp.float32, jnp.bfloat16
    c, h, r = lax.axis_index("ctx"), lax.axis_index("head"), lax.axis_index("roll")
    other = 1 - c
    sib = r + 1 - 2 * lax.rem(r, 2)
    far = lax.rem(r + 2, 4)
    far_sib = lax.rem(sib + 2, 4)
    partner = {"ctx": other}
    rows, head_size = qbuf.shape[1], qbuf.shape[2]
    half = rows // 2
    slots = kbuf.shape[1]
    factor = math.log2(math.e) / math.sqrt(head_size)

    barrier = pltpu.get_barrier_semaphore()
    peers = [partner, {"roll": sib}, {"roll": far}, {"ctx": other, "roll": far}]
    peers += [{"head": lax.rem(h + off, n_head)} for off in range(1, n_head)]
    for peer in peers:
        pl.semaphore_signal(barrier, inc=1, device_id=peer, device_id_type=MESH)

    local = {}

    def fetch(name, src, dst, sem):
        local[name] = pltpu.make_async_copy(src, dst, sem)
        local[name].start()

    mine = pl.ds(pl.multiple_of(c * half, half), half)
    fetch("q", q_hbm.at[0], qbuf.at[:, mine, :], q_sem)
    fetch("k0", k_hbm.at[0, other], kbuf.at[other], k_sem.at[0])
    fetch("v0", v_hbm.at[0, other], vbuf.at[other], v_sem.at[0])
    fetch("pos", pos_hbm, pos_ref, n_sem)
    fetch("k1", k_hbm.at[0, c], kbuf.at[c], k_sem.at[1])
    fetch("v1", v_hbm.at[0, c], vbuf.at[c], v_sem.at[1])
    fetch("fk", fk_hbm.at[0, c], fkbuf, f_sem.at[0])
    fetch("fv", fv_hbm.at[0, c], fvbuf, f_sem.at[1])

    pl.semaphore_wait(barrier, len(peers))

    q_copies = []
    for at, head in enumerate((c, other)):
        q_copies.append(
            pltpu.make_async_remote_copy(
                src_ref=q_hbm.at[0, head],
                dst_ref=qbuf.at[head, mine, :],
                send_sem=qx_send.at[at],
                recv_sem=qx_recv.at[at],
                device_id=partner,
                device_id_type=MESH,
            )
        )
        q_copies[-1].start()

    depth = w_hbm.shape[0] // 2
    for at, head in enumerate((c, other)):
        for cut in range(wbuf.shape[2] // WIDE):
            span = pl.ds(cut * WIDE, WIDE)
            fetch(
                ("w", at, cut),
                w_hbm.at[pl.ds(pl.multiple_of(head * depth, depth), depth), span],
                wbuf.at[head, :, span],
                w_sem.at[at, cut],
            )

    local["pos"].wait()
    length = len_ref[0]
    first_slot = c * slots

    def scores(query, head):
        fold = jnp.full((query.shape[0], 128), NEG, f32)
        for at in range(slots // CHUNK):
            span = slice(at * CHUNK, (at + 1) * CHUNK)
            part = lax.dot_general(
                query, kbuf[head, span, :], (((1,), (1,)), ((), ())), preferred_element_type=f32
            )
            slot = first_slot + at * CHUNK + lax.broadcasted_iota(jnp.int32, (1, CHUNK), 1)
            part = part + jnp.where(slot < length, 0.0, NEG)
            sbuf[0 : query.shape[0], span] = part
            for lane in range(CHUNK // 128):
                fold = jnp.maximum(fold, part[:, lane * 128 : (lane + 1) * 128])
        return jnp.max(fold, axis=1, keepdims=True)

    def weighted(count, head, top):
        ones = jnp.ones((CHUNK, 128), bf16)
        acc = jnp.zeros((count, head_size + 128), f32)
        for at in range(slots // CHUNK):
            span = slice(at * CHUNK, (at + 1) * CHUNK)
            weights = jnp.exp2((sbuf[0:count, span] - top) * factor).astype(bf16)
            both = jnp.concatenate([vbuf[head, span, :], ones], axis=1)
            acc = acc + jnp.dot(weights, both, preferred_element_type=f32)
        return acc[:, :head_size], acc[:, head_size:]

    lane = lax.broadcasted_iota(jnp.int32, (half, 128), 1)
    p_copies, s_copies = [], []

    def give_back(at, side):
        query = qbuf[other, pl.ds(pl.multiple_of(side * half, half), half), :]
        top = scores(query, other)
        if at == 0:
            local["v0"].wait()
        summed, total = weighted(half, other, top)
        po_send[side] = summed.astype(bf16)
        p_copies.append(
            pltpu.make_async_remote_copy(
                src_ref=po_send.at[side], dst_ref=po_recv.at[side],
                send_sem=px_send.at[at], recv_sem=px_recv.at[at],
                device_id=partner, device_id_type=MESH,
            )
        )
        p_copies[-1].start()
        turned = jnp.transpose(jnp.where(lane < 64, jnp.broadcast_to(top, (half, 128)), total))
        st_send[side, 0:8, :] = turned[0:8, :]
        st_send[side, 8:16, :] = turned[64:72, :]
        s_copies.append(
            pltpu.make_async_remote_copy(
                src_ref=st_send.at[side], dst_ref=st_recv.at[side],
                send_sem=sx_send.at[at], recv_sem=sx_recv.at[at],
                device_id=partner, device_id_type=MESH,
            )
        )
        s_copies[-1].start()

    token_here = lax.broadcasted_iota(jnp.int32, (half, NEW), 0) // QPK
    fresh_at = lax.broadcasted_iota(jnp.int32, (half, NEW), 1)

    def new_mask(side):
        token = token_here + side * (half // QPK)
        row_pos = jnp.zeros((half, NEW), jnp.int32)
        new_pos = jnp.zeros((half, NEW), jnp.int32)
        for t in range(NEW):
            value = pos_ref[0, t]
            row_pos = jnp.where(token == t, value, row_pos)
            new_pos = jnp.where(fresh_at == t, value, new_pos)
        return new_pos <= row_pos

    def keep(at, side, allow):
        query = qbuf[c, pl.ds(pl.multiple_of(side * half, half), half), :]
        top = scores(query, c)
        fresh = lax.dot_general(
            query, fkbuf[...], (((1,), (1,)), ((), ())), preferred_element_type=f32
        )
        fresh = jnp.where(allow, fresh, NEG)
        top = jnp.maximum(top, jnp.max(fresh, axis=1, keepdims=True))
        if at == 0:
            local["v1"].wait()
            local["fv"].wait()
        summed, total = weighted(half, c, top)
        fresh_weights = jnp.where(allow, jnp.exp2((fresh - top) * factor), 0.0).astype(bf16)
        summed = summed + jnp.dot(fresh_weights, fvbuf[...], preferred_element_type=f32)
        total = total + jnp.sum(fresh_weights.astype(f32), axis=1, keepdims=True)
        return jnp.broadcast_to(top, (half, 128)), total, summed

    def merge(side, state):
        top_here, total, summed = state
        top_there = jnp.transpose(jnp.broadcast_to(st_recv[side, 0:1, :], (128, half)))
        total_there = jnp.transpose(jnp.broadcast_to(st_recv[side, 8:9, :], (128, half)))
        best = jnp.maximum(top_here, top_there)
        here = jnp.exp2((top_here - best) * factor)
        there = jnp.exp2((top_there - best) * factor)
        num = summed * here + po_recv[side].astype(f32) * there
        den = total * here + total_there * there
        fbuf[pl.ds(pl.multiple_of(side * half, half), half), :] = num / den

    local["q"].wait()
    local["k0"].wait()
    give_back(0, c)
    local["k1"].wait()
    local["fk"].wait()
    state_mine = keep(0, c, new_mask(c))
    mask_other = new_mask(other)
    q_copies[0].wait_recv()
    give_back(1, other)
    q_copies[1].wait_recv()
    state_other = keep(1, other, mask_other)

    s_copies[0].wait_recv()
    p_copies[0].wait_recv()
    merge(other, state_other)
    s_copies[1].wait_recv()
    p_copies[1].wait_recv()
    merge(c, state_mine)
    for j in range(QPK):
        feature = fbuf[pl.ds(j, NEW, stride=QPK), :]
        gather[c, r, :, j * head_size : (j + 1) * head_size] = feature.astype(bf16)

    def pass_on(at, slot_c, slot_r, peer):
        block = gather.at[slot_c, slot_r]
        copy = pltpu.make_async_remote_copy(
            src_ref=block, dst_ref=block,
            send_sem=g_send.at[at], recv_sem=g_recv.at[at],
            device_id=peer, device_id_type=MESH,
        )
        copy.start()
        return copy

    g_far = pass_on(0, c, r, {"roll": far})
    g_sib = pass_on(1, c, r, {"roll": sib})
    g_ctx = pass_on(2, c, r, partner)
    g_diag = pass_on(3, c, r, {"ctx": other, "roll": far})
    g_far.wait_recv()
    f_far = pass_on(4, c, far, {"roll": sib})
    g_ctx.wait_recv()
    f_ctx = pass_on(5, other, r, {"roll": sib})
    g_sib.wait_recv()
    f_far.wait_recv()

    n_cols = wbuf.shape[2] // COLS
    tokens = gather.shape[1] * NEW

    def project(head, at, step):
        features = gather[head].reshape(tokens, depth)
        return jnp.dot(
            features, wbuf[head, :, at * step : (at + 1) * step], preferred_element_type=f32
        )

    f_diag = None
    n_wide = wbuf.shape[2] // WIDE
    for at in range(n_wide):
        local[("w", 0, at)].wait()
        accbuf[:, at * WIDE : (at + 1) * WIDE] = project(c, at, WIDE)
        if at == n_wide // 2 - 1:
            g_diag.wait_recv()
            f_diag = pass_on(6, other, far, {"roll": sib})
    f_ctx.wait_recv()
    f_diag.wait_recv()

    rs_copies = []
    for at in range(n_cols):
        span = slice(at * COLS, (at + 1) * COLS)
        if at * COLS % WIDE == 0:
            local[("w", 1, at * COLS // WIDE)].wait()
        part = accbuf[:, span] + project(other, at, COLS)
        accbuf[:, span] = part
        rs_send[:, :, span] = part.astype(bf16).reshape(n_head, NEW, COLS)
        for off in range(n_head - 1, 0, -1):
            to = lax.rem(h + off, n_head)
            copy = pltpu.make_async_remote_copy(
                src_ref=rs_send.at[to, :, span],
                dst_ref=rs_recv.at[off - 1, :, span],
                send_sem=rs_send_sem.at[off - 1, at],
                recv_sem=rs_recv_sem.at[off - 1, at],
                device_id={"head": to},
                device_id_type=MESH,
            )
            copy.start()
            rs_copies.append((at, copy))

    own = pl.ds(pl.multiple_of(h * NEW, NEW), NEW)
    for at in range(n_cols):
        span = slice(at * COLS, (at + 1) * COLS)
        for place, copy in rs_copies:
            if place == at:
                copy.wait_recv()
        value = accbuf[own, span]
        for off in range(n_head - 1):
            value = value + rs_recv[off, :, span].astype(f32)
        out_ref[0, :, span] = value.astype(bf16)

    for copy in q_copies + p_copies + s_copies:
        copy.wait_send()
    for copy in (g_far, g_sib, g_ctx, g_diag, f_far, f_ctx, f_diag):
        copy.wait_send()
    for _, copy in rs_copies:
        copy.wait_send()


def fused_body(n_head, queries, cache_keys, cache_values, new_keys, new_values, lengths, positions, out_weight):
    f32, bf16 = jnp.float32, jnp.bfloat16
    _, heads, slots, head_size = cache_keys.shape
    half = queries.shape[2]
    rows = 2 * half
    width = out_weight.shape[1]
    depth = out_weight.shape[0] // heads
    n_cols = width // COLS
    dma = pltpu.SemaphoreType.DMA
    pinned = [
        pltpu.with_memory_space_constraint(array, pltpu.HBM)
        for array in (queries, cache_keys, cache_values, new_keys, new_values, positions)
    ]
    anywhere = pl.BlockSpec(memory_space=pltpu.HBM)
    return pl.pallas_call(
        functools.partial(fused_kernel, n_head),
        out_shape=jax.ShapeDtypeStruct((1, NEW, width), bf16),
        in_specs=[anywhere] * 5 + [pl.BlockSpec(memory_space=pltpu.SMEM)] + [anywhere] * 2,
        out_specs=pl.BlockSpec(memory_space=pltpu.VMEM),
        scratch_shapes=[
            pltpu.SMEM(positions.shape, positions.dtype),
            pltpu.VMEM((heads, rows, head_size), bf16),
            pltpu.VMEM((heads, slots, head_size), bf16),
            pltpu.VMEM((heads, slots, head_size), bf16),
            pltpu.VMEM((NEW, head_size), bf16),
            pltpu.VMEM((NEW, head_size), bf16),
            pltpu.VMEM((heads, depth, width), bf16),
            pltpu.VMEM((half, slots), f32),
            pltpu.VMEM((2, half, head_size), bf16),
            pltpu.VMEM((2, half, head_size), bf16),
            pltpu.VMEM((2, 16, half), f32),
            pltpu.VMEM((2, 16, half), f32),
            pltpu.VMEM((rows, head_size), f32),
            pltpu.VMEM((2, 4, NEW, depth), bf16),
            pltpu.VMEM((4 * NEW, width), f32),
            pltpu.VMEM((n_head, NEW, width), bf16),
            pltpu.VMEM((n_head - 1, NEW, width), bf16),
            dma, dma((2,)), dma((2,)), dma((2,)), dma, dma((2, width // WIDE)),
            dma((2,)), dma((2,)), dma((2,)), dma((2,)), dma((2,)), dma((2,)),
            dma((7,)), dma((7,)),
            dma((n_head - 1, n_cols)), dma((n_head - 1, n_cols)),
        ],
        compiler_params=pltpu.CompilerParams(
            collective_id=0, has_side_effects=True, vmem_limit_bytes=48 * 1024 * 1024
        ),
        cost_estimate=pl.CostEstimate(
            flops=4 * heads * rows * slots * head_size + 2 * 4 * NEW * heads * depth * width,
            bytes_accessed=2 * heads * (2 * slots * head_size + depth * width),
            transcendentals=heads * rows * slots,
        ),
    )(*pinned[:5], lengths, pinned[5], out_weight)


def shifted(value, axis, steps):
    count = lax.axis_size(axis)
    pairs = [(source, (source + steps) % count) for source in range(count)]
    return lax.ppermute(value, axis, pairs)


def ring_body(queries, cache_keys, cache_values, new_keys, new_values, lengths, positions, out_weight):
    here = lax.axis_index("ctx")
    n_ctx = lax.axis_size("ctx")
    slots = cache_keys.shape[2]
    head_size = cache_keys.shape[3]
    local_heads = cache_keys.shape[1]
    scale = 1.0 / head_size**0.5
    keys = cache_keys[0]
    values = cache_values[0]
    fresh_keys = new_keys[0]
    fresh_values = new_values[0]
    pos = positions[0]
    slot_ok = here * slots + jnp.arange(slots) < lengths[0]

    def update(state, block, first_row, use_new):
        top_old, total_old, summed_old = state
        count = block.shape[1]
        scores = jnp.einsum("krd,ksd->krs", block, keys, preferred_element_type=jnp.float32) * scale
        scores = jnp.where(slot_ok[None, None, :], scores, NEG)
        fresh = (
            jnp.einsum("krd,kud->kru", block, fresh_keys, preferred_element_type=jnp.float32)
            * scale
        )
        token = (first_row + jnp.arange(count)) // QPK
        allow = jnp.logical_and(pos[None, :] <= pos[token][:, None], use_new)
        fresh = jnp.where(allow[None], fresh, NEG)
        top = jnp.maximum(top_old, jnp.maximum(jnp.max(scores, axis=2), jnp.max(fresh, axis=2)))
        cache_weights = jnp.where(
            slot_ok[None, None, :], jnp.exp(scores - top[..., None]), 0.0
        ).astype(jnp.bfloat16)
        fresh_weights = jnp.where(allow[None], jnp.exp(fresh - top[..., None]), 0.0).astype(
            jnp.bfloat16
        )
        factor = jnp.exp(top_old - top)
        total = total_old * factor + jnp.sum(cache_weights.astype(jnp.float32), axis=2)
        total = total + jnp.sum(fresh_weights.astype(jnp.float32), axis=2)
        summed = summed_old * factor[..., None]
        summed = summed + jnp.einsum(
            "krs,ksd->krd", cache_weights, values, preferred_element_type=jnp.float32
        )
        summed = summed + jnp.einsum(
            "kru,kud->krd", fresh_weights, fresh_values, preferred_element_type=jnp.float32
        )
        return (top, total, summed)

    block = queries[0]
    block_rows = block.shape[1]
    state = update(
        (
            jnp.full((local_heads, block_rows), NEG, jnp.float32),
            jnp.zeros((local_heads, block_rows), jnp.float32),
            jnp.zeros((local_heads, block_rows, head_size), jnp.float32),
        ),
        block,
        here * block_rows,
        True,
    )

    def turn(step, carry):
        moving, top, total, summed = carry
        moving = shifted(moving, "ctx", 1)
        top, total, summed = shifted((top, total, summed), "ctx", 1)
        top, total, summed = update((top, total, summed), moving, 0, False)
        return (moving, top, total, summed)

    moving, top, total, summed = lax.fori_loop(
        0, n_ctx - 1, turn, (block, state[0], state[1], state[2])
    )
    attended = (summed / total[..., None]).astype(jnp.bfloat16)
    every = lax.all_gather(attended[None], ("ctx", "roll"), axis=0, tiled=True)
    n_roll = every.shape[0] // n_ctx
    every = every.reshape(n_ctx, n_roll, local_heads, block_rows, head_size)
    every = jnp.roll(every, 1, axis=0)
    rows_all = every.transpose(1, 2, 0, 3, 4).reshape(
        n_roll, local_heads, n_ctx * block_rows, head_size
    )
    n_roll = rows_all.shape[0]
    features = rows_all.reshape(n_roll, local_heads, NEW, QPK, head_size).transpose(0, 2, 1, 3, 4)
    features = features.reshape(n_roll, NEW, local_heads * QPK * head_size)
    return lax.psum_scatter(
        jnp.einsum("rtf,fc->rtc", features, out_weight, preferred_element_type=jnp.float32).astype(
            jnp.bfloat16
        ),
        "head",
        scatter_dimension=0,
        tiled=True,
    )


def solution(mesh):
    in_specs = (
        P("roll", "head", "ctx", None),
        P("roll", "head", "ctx", None),
        P("roll", "head", "ctx", None),
        P("roll", "head", None, None),
        P("roll", "head", None, None),
        P("roll"),
        P("roll", None),
        P("head", ("ctx", "roll")),
    )
    out_specs = P("head", None, ("ctx", "roll"))
    body = ring_body
    if (mesh.shape["ctx"], mesh.shape["head"], mesh.shape["roll"]) == (2, 4, 4):
        body = functools.partial(fused_body, mesh.shape["head"])
    return jax.shard_map(body, mesh=mesh, in_specs=in_specs, out_specs=out_specs, check_vma=False)
```
